128 devices in a mesh: hull: 8 (over y, core), blk: 16 (over x, z).
Axes of the slice: x: 4, y: 4, z: 4, core: 2. Of those that a mesh axis runs over, the one named last changes fastest.
Arguments:
- source: float32 [7, 64, 32768], P(None, 'hull', 'blk'), may hold values from -500 to 500
- jacobian: float32 [7, 7, 64, 32768], P(None, None, 'hull', 'blk'), may hold values from -0.03 to 0.5, as said below
- face_coef: float32 [4, 7, 64, 32768], P(None, None, 'hull', 'blk'), may hold values from 0.1 to 1.5
- active: int32 [64, 32768], P('hull', 'blk'), may hold values 0 or 1
Outputs:
- adjoint: float32 [7, 64, 32768], P(None, 'hull', 'blk')
- residual: float32 [7, 64, 32768], P(None, 'hull', 'blk')
- level_rms: float32 [3], replicated
The draws below stay inside these ranges and needn't reach their ends.
Inputs may be any that keep to these rules, and one draw needn't show every extreme that they name: `jacobian`: in each tile the diagonal entry exceeds the sum of magnitudes of the other entries of its row.
All inputs are finite; a program needn't handle non-finite values. No bound on the sum of `active` on one device may be relied on, other than what follows from the above.
Results may differ from the reference program's by a relative error of at most 0.0003.
Values sent between devices are 32-bit elements; how exact they have to be, the bound alone decides.
No kernel may reach another device: no remote copies, remote signals or barrier semaphores. Data moves between devices by JAX's collectives and lax.ppermute only.
A program may use at most 128 MiB of HBM per device.

```python
import jax
import jax.numpy as jnp

F = 7
CB = 2048
LEVELS = 2
SWEEPS = 2
COARSE_SWEEPS = 4
NA = 64
NB = 32768


def draw_source(key, part):
    key = jax.random.fold_in(key, 11)
    key_base, key_rows, key_cols = jax.random.split(key, 3)
    base = jnp.clip(jax.random.normal(key_base, (F, NA, NB), jnp.float32), -4.0, 4.0)
    rise = 3.0
    row_scale = 10.0 ** jax.random.uniform(key_rows, (NA,), jnp.float32, 0.0, 0.6) * rise ** (jnp.arange(NA, dtype=jnp.float32) / NA)
    col_scale = 10.0 ** jax.random.uniform(key_cols, (NB,), jnp.float32, 0.0, 0.6) * rise ** (jnp.arange(NB, dtype=jnp.float32) / NB)
    return 0.15 * base * row_scale[None, :, None] * col_scale[None, None, :]


def draw_jacobian(key, part):
    key = jax.random.fold_in(key, 23)
    key_off, key_diag = jax.random.split(key)
    coupling = jax.random.uniform(key_off, (F, F, NA, NB), jnp.float32, -0.03, 0.03)
    leading = jax.random.uniform(key_diag, (F, NA, NB), jnp.float32, 0.2, 0.5)
    identity = jnp.eye(F, dtype=jnp.float32)[:, :, None, None]
    return coupling * (1.0 - identity) + identity * leading[None, :, :, :]


def draw_face_coef(key, part):
    key = jax.random.fold_in(key, 37)
    key_strong, key_weak = jax.random.split(key)
    shape = (4, F, NA, NB)
    strong = jnp.exp(jax.random.uniform(key_strong, shape, jnp.float32, jnp.log(0.75), jnp.log(1.5)))
    weak = jnp.exp(jax.random.uniform(key_weak, shape, jnp.float32, jnp.log(0.1), jnp.log(0.2)))
    position = jnp.arange(NB, dtype=jnp.int32) % CB
    near_edge = jnp.where((position < CB // 4) | (position >= CB - CB // 4), 1.0, 0.0).astype(jnp.float32)
    along = jnp.array([1.0, 1.0, 0.0, 0.0], jnp.float32)[:, None, None, None]
    edge_cols = near_edge[None, None, None, :]
    high = along * edge_cols + (1.0 - along) * (1.0 - edge_cols)
    return high * strong + (1.0 - high) * weak


def place_ends(entries, rng, least, top_value):
    place = [jax.random.randint(jax.random.fold_in(rng, axis), (), 0, length) for axis, length in enumerate(entries.shape)]
    widest = entries.shape.index(max(entries.shape))
    next_to = place[:widest] + [(place[widest] + 1) % entries.shape[widest]] + place[widest + 1:]
    return entries.at[tuple(place)].set(least).at[tuple(next_to)].set(top_value)


def setup_inputs(seed: int = 0) -> dict:
    key_list = jax.random.split(jax.random.key(seed), 5)
    return {
        "source": draw_source(jax.random.fold_in(key_list[4], 71), 0),
        "jacobian": draw_jacobian(jax.random.fold_in(key_list[4], 71), 0),
        "face_coef": draw_face_coef(jax.random.fold_in(key_list[4], 71), 0),
        "active": place_ends((jax.random.randint(key_list[3], (NA, NB), 0, 8) < 7).astype(jnp.int32), jax.random.fold_in(key_list[3], 1), 0, 1),
    }


damping = 0.7

def pad_axis(array, axis, before, after):
    widths = [(0, 0)] * array.ndim
    widths[array.ndim + axis] = (before, after)
    return jnp.pad(array, widths)

def couplings(face_coef):
    east = pad_axis(face_coef[0][..., :-1], -1, 1, 0)
    west = pad_axis(face_coef[1][..., 1:], -1, 0, 1)
    north = pad_axis(face_coef[2][..., :-1, :], -2, 1, 0)
    south = pad_axis(face_coef[3][..., 1:, :], -2, 0, 1)
    face_sum = face_coef[0] + face_coef[1] + face_coef[2] + face_coef[3]
    return jnp.stack([face_sum, east, west, north, south])

def apply_adjoint(vector, jacobian, couple):
    result = couple[0] * vector
    result = result - couple[1] * pad_axis(vector[..., :-1], -1, 1, 0)
    result = result - couple[2] * pad_axis(vector[..., 1:], -1, 0, 1)
    result = result - couple[3] * pad_axis(vector[..., :-1, :], -2, 1, 0)
    result = result - couple[4] * pad_axis(vector[..., 1:, :], -2, 0, 1)
    for field in range(jacobian.shape[0]):
        result = result + jacobian[field] * vector[field]
    return result

def diagonal_of(jacobian, couple):
    return jnp.stack([jacobian[field, field] for field in range(jacobian.shape[0])]) + couple[0]

def pair_sum(array):
    return array[..., 0::2] + array[..., 1::2]

def coarsen_couple(couple):
    even = couple[..., 0::2]
    odd = couple[..., 1::2]
    return jnp.stack([even[0] + odd[0] - even[2] - odd[1], even[1], odd[2], even[3] + odd[3], even[4] + odd[4]])

def expand(array):
    return jnp.repeat(array, 2, axis=-1)

def smooth(vector, target, jacobian, couple, diagonal):
    return vector + damping * (target - apply_adjoint(vector, jacobian, couple)) / diagonal

def reference(source, jacobian, face_coef, active):
    fields = source.shape[0]
    target = source
    jac_level = jacobian
    couple = couplings(face_coef)
    cell_mask = active.astype(jnp.float32)
    diagonal = diagonal_of(jac_level, couple)
    operators = [(jac_level, couple, diagonal)]
    targets = [target]
    adjoint = jnp.zeros(target.shape, jnp.float32)
    for sweep in range(SWEEPS):
        adjoint = smooth(adjoint, target, jac_level, couple, diagonal) * cell_mask
    residual = (target - apply_adjoint(adjoint, jac_level, couple)) * cell_mask
    squares = [jnp.sum(residual * residual)]
    corrections = [adjoint]
    for level in range(1, LEVELS + 1):
        jac_level = pair_sum(jac_level)
        couple = coarsen_couple(couple)
        diagonal = diagonal_of(jac_level, couple)
        level_target = pair_sum(residual)
        correction = jnp.zeros(level_target.shape, jnp.float32)
        count = SWEEPS if level < LEVELS else COARSE_SWEEPS
        for sweep in range(count):
            correction = smooth(correction, level_target, jac_level, couple, diagonal)
        operators.append((jac_level, couple, diagonal))
        targets.append(level_target)
        corrections.append(correction)
        if level < LEVELS:
            residual = level_target - apply_adjoint(correction, jac_level, couple)
            squares.append(jnp.sum(residual * residual) * 2.0 ** level)
    for level in range(LEVELS - 1, 0, -1):
        correction = corrections[level] + expand(corrections[level + 1])
        jac_level, couple, diagonal = operators[level]
        for sweep in range(SWEEPS):
            correction = smooth(correction, targets[level], jac_level, couple, diagonal)
        corrections[level] = correction
    jac_level, couple, diagonal = operators[0]
    adjoint = adjoint + expand(corrections[1]) * cell_mask
    for sweep in range(SWEEPS):
        adjoint = smooth(adjoint, target, jac_level, couple, diagonal) * cell_mask
    residual = (target - apply_adjoint(adjoint, jac_level, couple)) * cell_mask
    squares.append(jnp.sum(residual * residual))
    level_rms = jnp.sqrt(jnp.stack(squares) / float(fields * NA * NB))
    return (adjoint, residual, level_rms)
```

```python
import jax
import jax.numpy as jnp
from jax import lax
from jax.experimental import pallas as pl
from jax.experimental.pallas import tpu as pltpu
from jax.sharding import PartitionSpec as P

FIELDS = 7
ROWS = 8
WIDE = 2
T = 128
HALF = 64
DAMP = 0.7
PLANES = 12
SWEEP_W = 11
F32 = jnp.float32
LIMIT = 12 * 2**20


def iota(shape, dim):
    return lax.broadcasted_iota(jnp.int32, shape, dim)


def tile(j):
    return pl.ds(pl.multiple_of(j * T, T), T)


def each_tile(count, body):
    def step(j, carry):
        body(j)
        return carry

    lax.fori_loop(0, count, step, 0)


def swap(x, span):
    low = (iota(x.shape, 1) // span) % 2 == 0
    return jnp.where(low, pltpu.roll(x, T - span, 1), pltpu.roll(x, span, 1))


def lower_half(x, span):
    low = (iota(x.shape, 1) // span) % 2 == 0
    return jnp.where(low, x, pltpu.roll(x, span, 1))


def upper_half(x, span):
    low = (iota(x.shape, 1) // span) % 2 == 0
    return jnp.where(low, pltpu.roll(x, T - span, 1), x)


def diagonal(planes):
    sub = iota(planes[0].shape, 0)
    out = planes[FIELDS - 1]
    for f in range(FIELDS - 1):
        out = jnp.where(sub == f, planes[f], out)
    return out


def coarser(planes, span):
    low_j = [p + swap(p, span) for p in planes[:FIELDS]]
    f0, f1, f2, f3 = planes[FIELDS : FIELDS + 4]
    f0_low, f0_up = lower_half(f0, span), upper_half(f0, span)
    f1_low, f1_up = lower_half(f1, span), upper_half(f1, span)
    inner = f1_up + f0_low
    sub = iota(f0.shape, 0)
    low_j = [jnp.where(sub == f, p - inner, p) for f, p in enumerate(low_j)]
    return low_j + [f0_up, f1_low, f2 + swap(f2, span), f3 + swap(f3, span)]


def split_kernel(jac, face, src, act, c0, t0, top, bottom, left, right, buf):
    columns = src.shape[-1]
    last = columns // T - 1

    def body(j):
        sl = tile(j)
        for f in range(FIELDS):
            buf[f] = jac[f, :, sl]
        for k in range(4):
            buf[FIELDS + k] = face[k, :, sl]
        buf[PLANES - 1] = src[:, sl]
        for r in range(ROWS):
            pick = pl.ds(r, FIELDS, stride=ROWS)
            planes = [buf[f, pick, :] for f in range(FIELDS)]
            faces = [buf[FIELDS + k, pick, :] for k in range(4)]
            total = faces[0] + faces[1] + faces[2] + faces[3]
            sub = iota(total.shape, 0)
            planes = [jnp.where(sub == f, p + total, p) for f, p in enumerate(planes)]
            mask = act[r : r + 1, sl].astype(F32)
            for k, p in enumerate(planes + faces):
                c0[r + WIDE, k, 0:FIELDS, sl] = p
            c0[r + WIDE, SWEEP_W, 0:FIELDS, sl] = DAMP * mask / diagonal(planes)
            t0[r + WIDE, 0:FIELDS, sl] = buf[PLANES - 1, pick, :]
            t0[r + WIDE, FIELDS : FIELDS + 1, sl] = mask

    each_tile(columns // T, body)

    def rows(j):
        sl = tile(j)
        for out, first in ((top, 0), (bottom, ROWS - WIDE)):
            for w in range(WIDE):
                for k in range(PLANES - 1):
                    out[w, k, :, sl] = c0[first + w + WIDE, k, :, sl]
                out[w, PLANES - 1, :, sl] = t0[first + w + WIDE, :, sl]

    each_tile(columns // T, rows)

    def cols(r):
        for out, j in ((left, 0), (right, last)):
            sl = slice(j * T, j * T + T)
            for k in range(PLANES - 1):
                out[r, k] = c0[r + WIDE, k, :, sl]
            out[r, PLANES - 1] = t0[r + WIDE, :, sl]

    each_tile(ROWS, cols)


def build_levels(c0, c1, c2, r, sl, domain):
    planes = [c0[r, k, :, sl] for k in range(PLANES - 1)]
    for out, span in ((c1, 1), (c2, 2)):
        planes = coarser(planes, span)
        for k, p in enumerate(planes):
            out[r, k, :, sl] = p
        weight = DAMP / diagonal(planes[:FIELDS])
        out[r, SWEEP_W, :, sl] = weight if domain is None else weight * domain


def own_levels_kernel(c0, c1, c2):
    def body(j):
        for r in range(ROWS):
            build_levels(c0, c1, c2, r + WIDE, tile(j), None)

    each_tile(c0.shape[-1] // T - 1, body)


def side_domain(flags):
    lane = iota((8, T), 1)
    return jnp.where(lane < HALF, flags[3], flags[2])


def row_flag(flags, r):
    if r < WIDE:
        return flags[0]
    if r >= WIDE + ROWS:
        return flags[1]
    return None


HALO_ROWS = list(range(WIDE)) + list(range(WIDE + ROWS, 2 * WIDE + ROWS))


def halo_levels_kernel(flags, c0, c1_in, c2_in, c1, c2):
    tiles = c0.shape[-1] // T

    def body(j):
        for r in HALO_ROWS:
            build_levels(c0, c1, c2, r, tile(j), row_flag(flags, r))

    each_tile(tiles - 1, body)
    sides = side_domain(flags)
    sl = slice((tiles - 1) * T, tiles * T)
    for r in range(2 * WIDE + ROWS):
        flag = row_flag(flags, r)
        build_levels(c0, c1, c2, r, sl, sides if flag is None else sides * flag)


def apply_at(c, r, v, vi, j, tiles, span, above=None, below=None):
    sl = tile(j)
    before = tile(lax.rem(j + tiles - 1, tiles))
    after = tile(lax.rem(j + 1, tiles))
    lane = iota((8, T), 1)
    here = v[vi, :, sl]
    out = c[r, 0, :, sl] * v[vi, 0:1, sl]
    for f in range(1, FIELDS):
        out = out + c[r, f, :, sl] * v[vi, f : f + 1, sl]
    k = FIELDS
    from_left = jnp.where(lane >= T - span, c[r, k, :, before] * v[vi, :, before], c[r, k, :, sl] * here)
    out = out - pltpu.roll(from_left, span, 1)
    from_right = jnp.where(lane < span, c[r, k + 1, :, after] * v[vi, :, after], c[r, k + 1, :, sl] * here)
    out = out - pltpu.roll(from_right, T - span, 1)
    out = out - (c[r - 1, k + 2, :, sl] * v[vi - 1, :, sl] if above is None else above)
    out = out - (c[r + 1, k + 3, :, sl] * v[vi + 1, :, sl] if below is None else below)
    return out


def first_kernel(flags, c0_in, t0_in, rows_above, rows_below, side, side_above, side_below, c0, t0, v2, t1, t1_top, t1_bottom, sums, va, vb):
    tiles = c0.shape[-1] // T
    last = slice((tiles - 1) * T, tiles * T)

    def put(r, planes, sl, domain):
        for k in range(PLANES - 1):
            c0[r, k, :, sl] = planes[k]
        source = planes[PLANES - 1]
        t0[r, :, sl] = source
        weight = DAMP * source[FIELDS : FIELDS + 1] / diagonal(planes[:FIELDS])
        weight = weight if domain is None else jnp.where(domain > 0.0, weight, 0.0)
        c0[r, SWEEP_W, :, sl] = weight
        va[r, :, sl] = weight * source

    def fill(j):
        sl = tile(j)
        for w in range(WIDE):
            put(w, [rows_above[w, k, :, sl] for k in range(PLANES)], sl, flags[0])
            put(WIDE + ROWS + w, [rows_below[w, k, :, sl] for k in range(PLANES)], sl, flags[1])
        for r in range(WIDE, WIDE + ROWS):
            va[r, :, sl] = c0[r, SWEEP_W, :, sl] * t0[r, :, sl]

    each_tile(tiles - 1, fill)
    sides = side_domain(flags)
    for r in range(ROWS):
        put(r + WIDE, [side[r, k] for k in range(PLANES)], last, sides)
    for w in range(WIDE):
        put(w, [side_above[w, k] for k in range(PLANES)], last, sides * flags[0])
        put(WIDE + ROWS + w, [side_below[w, k] for k in range(PLANES)], last, sides * flags[1])

    def sweep(j):
        sl = tile(j)
        for r in range(1, ROWS + 2 * WIDE - 1):
            diff = t0[r, :, sl] - apply_at(c0, r, va, r, j, tiles, 1)
            vb[r, :, sl] = va[r, :, sl] + diff * c0[r, SWEEP_W, :, sl]

    each_tile(tiles, sweep)
    sums[...] = jnp.zeros_like(sums)

    def rest(j):
        sl = tile(j)
        total = jnp.zeros((8, T), F32)
        for r in range(WIDE, WIDE + ROWS):
            diff = t0[r, :, sl] - apply_at(c0, r, vb, r, j, tiles, 1)
            res = jnp.where(c0[r, SWEEP_W, :, sl] != 0.0, diff, 0.0)
            total = total + res * res
            t1[r - WIDE, :, sl] = res + swap(res, 1)
            v2[r - WIDE, :, sl] = vb[r, :, sl]
        sums[...] += jnp.where(j < tiles - 1, total, 0.0)

    each_tile(tiles, rest)
    t1_top[...] = t1[0:WIDE]
    t1_bottom[...] = t1[ROWS - WIDE : ROWS]


def second_kernel(c1, c2, t1_own, t1_above, t1_below, t1, e1, t2, send_top, send_bottom, sums, va, vb):
    tiles = c1.shape[-1] // T

    def fill(j):
        sl = tile(j)
        for r in range(ROWS + 2 * WIDE):
            if r < WIDE:
                val = t1_above[r, :, sl]
            elif r < WIDE + ROWS:
                val = t1_own[r - WIDE, :, sl]
            else:
                val = t1_below[r - WIDE - ROWS, :, sl]
            t1[r, :, sl] = val
            va[r, :, sl] = c1[r, SWEEP_W, :, sl] * val

    each_tile(tiles, fill)

    def sweep(j):
        sl = tile(j)
        for r in range(1, ROWS + 2 * WIDE - 1):
            diff = t1[r, :, sl] - apply_at(c1, r, va, r, j, tiles, 2)
            vb[r, :, sl] = va[r, :, sl] + diff * c1[r, SWEEP_W, :, sl]

    each_tile(tiles, sweep)
    sums[...] = jnp.zeros_like(sums)

    def rest(j):
        sl = tile(j)
        total = jnp.zeros((8, T), F32)
        for r in range(WIDE, WIDE + ROWS):
            res = t1[r, :, sl] - apply_at(c1, r, vb, r, j, tiles, 2)
            total = total + res * res
            val = res + swap(res, 2)
            t2[r - WIDE, :, sl] = val
            e1[r - WIDE, :, sl] = vb[r, :, sl]
            row = r - WIDE
            if row < WIDE:
                send_top[row, :, sl] = val
            if row == WIDE:
                send_top[WIDE, :, sl] = c2[r, FIELDS + 3, :, sl] * c2[r, SWEEP_W, :, sl] * val
            if row == ROWS - WIDE - 1:
                send_bottom[WIDE, :, sl] = c2[r, FIELDS + 2, :, sl] * c2[r, SWEEP_W, :, sl] * val
            if row >= ROWS - WIDE:
                send_bottom[row - ROWS + WIDE, :, sl] = val
        sums[...] += jnp.where(j < tiles - 1, total, 0.0)

    each_tile(tiles, rest)


def third_kernel(c2, t2_own, above, below, e1_in, e1, send_top, send_bottom, t2, va, vb):
    tiles = c2.shape[-1] // T
    high = ROWS + 2 * WIDE

    def fill(j):
        sl = tile(j)
        for r in range(high):
            if r < WIDE:
                val = above[r, :, sl]
            elif r < WIDE + ROWS:
                val = t2_own[r - WIDE, :, sl]
            else:
                val = below[r - WIDE - ROWS, :, sl]
            t2[r, :, sl] = val
            va[r, :, sl] = c2[r, SWEEP_W, :, sl] * val

    each_tile(tiles, fill)

    def value(j, r, v):
        sl = tile(j)
        up = above[WIDE, :, sl] if r == 0 else None
        down = below[WIDE, :, sl] if r == high - 1 else None
        diff = t2[r, :, sl] - apply_at(c2, r, v, r, j, tiles, 4, up, down)
        return v[r, :, sl] + diff * c2[r, SWEEP_W, :, sl]

    def sweep2(j):
        for r in range(high):
            vb[r, :, tile(j)] = value(j, r, va)

    def sweep3(j):
        for r in range(1, high - 1):
            va[r, :, tile(j)] = value(j, r, vb)

    def sweep4(j):
        sl = tile(j)
        for r in range(WIDE, WIDE + ROWS):
            row = r - WIDE
            val = e1_in[row, :, sl] + value(j, r, va)
            e1[row, :, sl] = val
            if row < WIDE:
                send_top[row, :, sl] = val
            if row >= ROWS - WIDE:
                send_bottom[row - ROWS + WIDE, :, sl] = val

    each_tile(tiles, sweep2)
    each_tile(tiles, sweep3)
    each_tile(tiles, sweep4)


def fourth_kernel(c1, c0, t1, e1, above, below, v2, v, send_top, send_bottom, va, vb):
    tiles = c1.shape[-1] // T

    def fill(j):
        sl = tile(j)
        for r in range(ROWS + 2 * WIDE):
            if WIDE <= r < WIDE + ROWS:
                va[r, :, sl] = e1[r - WIDE, :, sl]
            else:
                val = above[r, :, sl] if r < WIDE else below[r - WIDE - ROWS, :, sl]
                va[r, :, sl] = jnp.where(c1[r, SWEEP_W, :, sl] != 0.0, val, 0.0)

    each_tile(tiles, fill)

    def value(j, r, x):
        sl = tile(j)
        diff = t1[r, :, sl] - apply_at(c1, r, x, r, j, tiles, 2)
        return x[r, :, sl] + diff * c1[r, SWEEP_W, :, sl]

    def sweep(j):
        for r in range(1, ROWS + 2 * WIDE - 1):
            vb[r, :, tile(j)] = value(j, r, va)

    def last(j):
        sl = tile(j)
        for r in range(WIDE, WIDE + ROWS):
            row = r - WIDE
            val = v2[row, :, sl] + jnp.where(c0[r, SWEEP_W, :, sl] != 0.0, value(j, r, vb), 0.0)
            v[row, :, sl] = val
            if row < WIDE:
                send_top[row, :, sl] = val
            if row == WIDE:
                send_top[WIDE, :, sl] = c0[r, FIELDS + 3, :, sl] * val
            if row == ROWS - WIDE - 1:
                send_bottom[WIDE, :, sl] = c0[r, FIELDS + 2, :, sl] * val
            if row >= ROWS - WIDE:
                send_bottom[row - ROWS + WIDE, :, sl] = val

    each_tile(tiles, sweep)
    each_tile(tiles, last)


def fifth_kernel(c0, t0, v, above, below, adjoint, residual, sums, va, vb, buf):
    tiles = c0.shape[-1] // T
    high = ROWS + 2 * WIDE

    def fill(j):
        sl = tile(j)
        for r in range(high):
            if WIDE <= r < WIDE + ROWS:
                va[r, :, sl] = v[r - WIDE, :, sl]
            else:
                val = above[r, :, sl] if r < WIDE else below[r - WIDE - ROWS, :, sl]
                va[r, :, sl] = jnp.where(c0[r, SWEEP_W, :, sl] != 0.0, val, 0.0)

    each_tile(tiles, fill)

    def value(j, r, x):
        sl = tile(j)
        up = above[WIDE, :, sl] if r == 0 else None
        down = below[WIDE, :, sl] if r == high - 1 else None
        diff = t0[r, :, sl] - apply_at(c0, r, x, r, j, tiles, 1, up, down)
        return x[r, :, sl] + diff * c0[r, SWEEP_W, :, sl]

    def sweep1(j):
        for r in range(high):
            vb[r, :, tile(j)] = value(j, r, va)

    def sweep2(j):
        for r in range(1, high - 1):
            va[r, :, tile(j)] = value(j, r, vb)

    each_tile(tiles, sweep1)
    each_tile(tiles, sweep2)
    sums[...] = jnp.zeros_like(sums)

    def rest(j):
        sl = tile(j)
        total = jnp.zeros((8, T), F32)
        for r in range(WIDE, WIDE + ROWS):
            diff = t0[r, :, sl] - apply_at(c0, r, va, r, j, tiles, 1)
            res = jnp.where(c0[r, SWEEP_W, :, sl] != 0.0, diff, 0.0)
            total = total + res * res
            pick = pl.ds(r - WIDE, FIELDS, stride=ROWS)
            buf[0, pick, :] = res[0:FIELDS]
            buf[1, pick, :] = va[r, 0:FIELDS, sl]
        residual[:, sl] = buf[0]
        adjoint[:, sl] = buf[1]
        sums[...] += total

    each_tile(tiles - 1, rest)


def call(kernel, outs, args, scratch=(), alias=None, flags=False, flops=0, size=0):
    vmem = pl.BlockSpec(memory_space=pltpu.VMEM)
    in_specs = [vmem] * len(args)
    if flags:
        in_specs[0] = pl.BlockSpec(memory_space=pltpu.SMEM)
    return pl.pallas_call(
        kernel,
        out_shape=[jax.ShapeDtypeStruct(s, F32) for s in outs],
        in_specs=in_specs,
        out_specs=[vmem] * len(outs),
        scratch_shapes=[pltpu.VMEM(s, F32) for s in scratch],
        input_output_aliases=alias or {},
        compiler_params=pltpu.CompilerParams(vmem_limit_bytes=LIMIT),
        cost_estimate=pl.CostEstimate(flops=flops, bytes_accessed=size, transcendentals=0),
        name=kernel.__name__,
    )(*args)


def ring(x, axis, step):
    count = lax.axis_size(axis)
    return lax.ppermute(x, axis, [(i, (i + step) % count) for i in range(count)])


def xor(x, axis, bits):
    count = lax.axis_size(axis)
    return lax.ppermute(x, axis, [(i, i ^ bits) for i in range(count)])


def total_over_devices(x):
    x = x + xor(x, "hull", 1)
    for axis, unit in (("hull", 2), ("blk", 1), ("blk", 4)):
        x = x + xor(x, axis, unit) + xor(x, axis, 2 * unit) + xor(x, axis, 3 * unit)
    return x


def on_device(source, jacobian, face_coef, active):
    columns = source.shape[2]
    wide = columns + T
    hull, blk = lax.axis_index("hull"), lax.axis_index("blk")
    flags = jnp.stack([hull > 0, hull < lax.axis_size("hull") - 1, blk > 0, blk < lax.axis_size("blk") - 1]).astype(F32)
    ext = ROWS + 2 * WIDE
    c_shape = (ext, PLANES, 8, wide)
    row_shape = (ext, 8, wide)
    own = (ROWS, 8, wide)
    two, three = (WIDE, 8, wide), (WIDE + 1, 8, wide)
    tile_shape = (8, T)

    c0, t0, top, bottom, left, right = call(
        split_kernel,
        [c_shape, row_shape, (WIDE, PLANES, 8, columns), (WIDE, PLANES, 8, columns), (ROWS, PLANES, 8, T), (ROWS, PLANES, 8, T)],
        [
            jacobian.reshape(FIELDS, FIELDS * ROWS, columns),
            face_coef.reshape(4, FIELDS * ROWS, columns),
            source.reshape(FIELDS * ROWS, columns),
            active,
        ],
        [(PLANES, FIELDS * ROWS, T)],
    )
    from_right = ring(left, "blk", -1)
    from_left = ring(right, "blk", 1)
    rows_below = ring(top, "hull", -1)
    rows_above = ring(bottom, "hull", 1)
    c1, c2 = call(own_levels_kernel, [c_shape, c_shape], [c0], size=10**7)
    side = jnp.where(lax.broadcasted_iota(jnp.int32, from_right.shape, 3) < HALF, from_right, from_left)
    side_below = ring(side[0:WIDE], "hull", -1)
    side_above = ring(side[ROWS - WIDE : ROWS], "hull", 1)
    c0, t0, v2, t1, t1_top, t1_bottom, sum0 = call(
        first_kernel,
        [c_shape, row_shape, own, own, two, two, tile_shape],
        [flags, c0, t0, rows_above, rows_below, side, side_above, side_below],
        [row_shape, row_shape],
        {1: 0, 2: 1},
        True,
    )
    t1_below = ring(t1_top, "hull", -1)
    t1_above = ring(t1_bottom, "hull", 1)
    c1, c2 = call(halo_levels_kernel, [c_shape, c_shape], [flags, c0, c1, c2], alias={2: 0, 3: 1}, flags=True, size=10**7)
    t1, e1, t2, send_top, send_bottom, sum1 = call(
        second_kernel, [row_shape, own, own, three, three, tile_shape], [c1, c2, t1, t1_above, t1_below], [row_shape, row_shape]
    )
    below = ring(send_top, "hull", -1)
    above = ring(send_bottom, "hull", 1)
    e1, send_top, send_bottom = call(
        third_kernel, [own, two, two], [c2, t2, above, below, e1], [row_shape] * 3
    )
    below = ring(send_top, "hull", -1)
    above = ring(send_bottom, "hull", 1)
    v, send_top, send_bottom = call(
        fourth_kernel, [own, three, three], [c1, c0, t1, e1, above, below, v2], [row_shape, row_shape]
    )
    below = ring(send_top, "hull", -1)
    above = ring(send_bottom, "hull", 1)
    adjoint, residual, sum2 = call(
        fifth_kernel, [(FIELDS * ROWS, columns)] * 2 + [tile_shape], [c0, t0, v, above, below],
        [row_shape, row_shape, (2, FIELDS * ROWS, T)],
    )
    squares = total_over_devices(jnp.stack([sum0, sum1, sum2]))
    squares = jnp.sum(squares[:, :FIELDS], axis=(1, 2))
    cells = source.size * lax.axis_size("hull") * lax.axis_size("blk")
    level_rms = jnp.sqrt(squares / float(cells))
    return adjoint.reshape(source.shape), residual.reshape(source.shape), level_rms


def solution(mesh):
    return jax.shard_map(
        on_device,
        mesh=mesh,
        in_specs=(
            P(None, "hull", "blk"),
            P(None, None, "hull", "blk"),
            P(None, None, "hull", "blk"),
            P("hull", "blk"),
        ),
        out_specs=(P(None, "hull", "blk"), P(None, "hull", "blk"), P()),
        check_vma=False,
    )
```

```python
import jax
import jax.numpy as jnp
from jax import lax
from jax.experimental import pallas as pl
from jax.experimental.pallas import tpu as pltpu
from jax.sharding import PartitionSpec as P

FIELDS = 7
ROWS = 8
WIDE = 2
EXT = ROWS + 2 * WIDE
T = 128
PHASES = 4
BLOCK = PHASES * T
SIDE = 8
SIDE_COLS = SIDE * PHASES
DAMP = 0.7
PLANES = 12
SWEEP_W = 11
SOURCE = 12
FINE = 13
F32 = jnp.float32
BF16 = jnp.bfloat16
LIMIT = 8 * 2**20
GRID = FIELDS * ROWS
RAW = PLANES * GRID
GROUPS = T // SIDE_COLS
PACK = RAW // GROUPS
PER_GROUP = PLANES // GROUPS


def iota(shape, dim):
    return lax.broadcasted_iota(jnp.int32, shape, dim)


def tile(j):
    return pl.ds(pl.multiple_of(j * T, T), T)


def each(count, body):
    def step(j, carry):
        body(j)
        return carry

    lax.fori_loop(0, count, step, 0)


class FineRows:
    def __init__(self, main, near, far=None):
        self.main, self.near, self.far = main, near, far
        self.shape = main.shape

    def __getitem__(self, at):
        r, *rest = at
        if r in (0, EXT - 1):
            return self.far[(r // (EXT - 1), *rest)]
        if r in (1, EXT - 2):
            return self.near[(r // (EXT - 2), *rest)]
        return self.main[(r - WIDE, *rest)]


class WithFar:
    def __init__(self, main, far):
        self.main, self.far = main, far
        self.shape = main.shape

    def __getitem__(self, at):
        r, *rest = at
        if r in (0, EXT - 1):
            return self.far[(r // (EXT - 1), *rest)]
        return self.main[(r, *rest)]


class SourceOf:
    def __init__(self, c):
        self.c = c

    def __getitem__(self, at):
        r, *rest = at
        return self.c[(r, SOURCE, *rest)]


def own_order():
    rows, cols = iota((BLOCK, BLOCK), 0), iota((BLOCK, BLOCK), 1)
    return jnp.where(rows == (cols % T) * PHASES + cols // T, 1.0, 0.0).astype(BF16)


def natural_order():
    rows, cols = iota((BLOCK, BLOCK), 0), iota((BLOCK, BLOCK), 1)
    return jnp.where(cols == (rows % T) * PHASES + rows // T, 1.0, 0.0).astype(BF16)


def side_order():
    rows, cols = iota((2 * T, BLOCK), 0), iota((2 * T, BLOCK), 1)
    lane, phase = cols % T, cols // T
    at = rows % SIDE_COLS
    after = (lane < SIDE) & (rows < T) & (at == lane * PHASES + phase)
    before = (lane >= T - SIDE) & (rows >= T) & (at == (lane - T + SIDE) * PHASES + phase)
    return jnp.where(after | before, 1.0, 0.0).astype(BF16)


def group_of(x, g):
    return jnp.where(iota(x.shape, 1) % T // SIDE_COLS == g, x, 0.0)


def reorder(x, order):
    high = x.astype(BF16)
    low = (x - high.astype(F32)).astype(BF16)
    return jnp.dot(high, order, preferred_element_type=F32) + jnp.dot(low, order, preferred_element_type=F32)


def diagonal(planes):
    sub = iota(planes[0].shape, 0)
    out = planes[FIELDS - 1]
    for f in range(FIELDS - 1):
        out = jnp.where(sub == f, planes[f], out)
    return out


def with_face_sum(planes, faces):
    total = faces[0] + faces[1] + faces[2] + faces[3]
    sub = iota(total.shape, 0)
    return [jnp.where(sub == f, x + total, x) for f, x in enumerate(planes)]


def weight_of(planes, mask):
    return jnp.where(mask > 0.0, DAMP / diagonal(planes), 0.0)


def fetch(jac, face, src, act, raw, flags, sems, columns):
    blocks = src.shape[-1] // columns

    def copies(b):
        cols = pl.ds(b * columns, columns)
        moves = [(jac.at[f, :, cols], raw.at[pl.ds(f * GRID, GRID), cols]) for f in range(FIELDS)]
        moves += [(face.at[k, :, cols], raw.at[pl.ds((FIELDS + k) * GRID, GRID), cols]) for k in range(4)]
        moves += [(src.at[:, cols], raw.at[pl.ds((PLANES - 1) * GRID, GRID), cols])]
        moves += [(act.at[:, cols], flags.at[:, cols])]
        return [pltpu.make_async_copy(a, d, sems.at[b, i]) for i, (a, d) in enumerate(moves)]

    todo = [copies(b) for b in range(blocks)]
    for group in todo:
        for copy in group:
            copy.start()

    def waiter(group):
        def wait():
            for copy in group:
                copy.wait()

        return wait

    return [waiter(group) for group in todo]


def send_kernel(jac, face, src, act, top, bottom, left, right, raw, flags, buf, sems):
    columns = src.shape[-1]
    waits = fetch(jac, face, src, act, raw, flags, sems, BLOCK)
    per = BLOCK // T

    def rows_of(b):
        def body(i):
            sl = tile(b * per + i)
            for k in range(PLANES):
                buf[k * GRID : k * GRID + GRID] = raw[k * GRID : k * GRID + GRID, sl]

            def pick(k, r):
                return buf[pl.ds(k * GRID + r, FIELDS, stride=ROWS), :]

            for out, near, far, face_k in ((top, 0, 1, 3), (bottom, ROWS - 1, ROWS - 2, 2)):
                for k in range(PLANES):
                    out[k, 0:FIELDS, sl] = pick(k, near)
                out[PLANES - 1, FIELDS : FIELDS + 1, sl] = flags[near : near + 1, sl].astype(F32)
                planes = [pick(k, far) for k in range(PLANES)]
                mask = flags[far : far + 1, sl].astype(F32)
                weight = weight_of(with_face_sum(planes[:FIELDS], planes[FIELDS : FIELDS + 4]), mask)
                out[PLANES, 0:FIELDS, sl] = planes[FIELDS + face_k] * weight * planes[PLANES - 1]
                for k in range(PLANES):
                    out[FINE + k, 0:FIELDS, sl] = planes[k]
                out[FINE + PLANES - 1, FIELDS : FIELDS + 1, sl] = mask

        each(per, body)

    for b, wait in enumerate(waits):
        wait()
        rows_of(b)
    lane = iota((PACK, T), 1) // SIDE_COLS
    for out, at, move in ((left, 0, 0), (right, columns - T, SIDE_COLS)):
        packed = None
        for g in range(GROUPS):
            part = raw[g * PACK : g * PACK + PACK, at : at + T]
            shift = (g * SIDE_COLS + move) % T
            part = pltpu.roll(part, shift, 1) if shift else part
            packed = part if packed is None else jnp.where(lane == g, part, packed)
        out[0:PACK] = packed
        mask = flags[:, at : at + T].astype(F32)
        out[PACK : PACK + ROWS] = pltpu.roll(mask, move, 1) if move else mask


def place(buf, masks, out, sl, domain):
    for r in range(ROWS):
        for p in range(PHASES):
            def pick(k):
                return buf[p, pl.ds(k * GRID + r, FIELDS, stride=ROWS), :]

            faces = [pick(FIELDS + k) for k in range(4)]
            planes = with_face_sum([pick(f) for f in range(FIELDS)], faces)
            mask = masks[p, r : r + 1, :]
            if domain is not None:
                mask = jnp.where(domain > 0.0, mask, 0.0)
            for k, x in enumerate(planes + faces + [weight_of(planes, mask), pick(PLANES - 1)]):
                out[r, k, p, 0:FIELDS, sl] = x


def side_domain(ends):
    lane = iota((1, T), 1)
    return jnp.where(lane < SIDE, ends[3], jnp.where(lane >= T - SIDE, ends[2], 0.0))


def corner_kernel(from_right, from_left, order_side, top, bottom):
    for side, packed in enumerate((from_right, from_left)):
        for out, rows in ((top, (0, 1)), (bottom, (ROWS - 1, ROWS - 2))):
            for i, r in enumerate(rows):
                for k in range(PER_GROUP):
                    out[i, side, k * 8 : k * 8 + FIELDS] = packed[pl.ds(k * GRID + r, FIELDS, stride=ROWS), :]
                out[i, side, FIELDS : FIELDS + 1] = packed[PACK + r : PACK + r + 1]


def corner_planes(corners, order):
    parts = [jnp.concatenate([c[i, 0], c[i, 1]], axis=1) for c in corners for i in range(2)]
    both = jnp.concatenate(parts, axis=0)
    size = PER_GROUP * 8
    packs = [reorder(group_of(both, g), order) for g in range(GROUPS)]
    result = []
    for n in range(len(parts)):
        def plane(k, p):
            first = n * size + k % PER_GROUP * 8
            return packs[k // PER_GROUP][first : first + 8, p * T : p * T + T]

        planes = [[plane(k, p) for p in range(PHASES)] for k in range(PLANES)]
        masks = [planes[0][p][FIELDS : FIELDS + 1] for p in range(PHASES)]
        result.append((planes, masks))
    return result


def side_kernel(ends, from_right, from_left, own, order, main, buf, masks, sems):
    inner = own.shape[-1]
    copies = [pltpu.make_async_copy(own.at[r], main.at[r, :, :, :, pl.ds(0, inner)], sems.at[r]) for r in range(ROWS)]
    for copy in copies:
        copy.start()
    both = jnp.concatenate([from_right[...], from_left[...]], axis=1)
    for g in range(GROUPS):
        x = reorder(group_of(both, g), order[...])
        for p in range(PHASES):
            buf[p, g * PACK : g * PACK + PACK] = x[0:PACK, p * T : p * T + T]
            if g == 0:
                masks[p] = x[PACK : PACK + ROWS, p * T : p * T + T]
    place(buf, masks, main, slice(inner, inner + T), side_domain(ends))
    for copy in copies:
        copy.wait()


def own_kernel(jac, face, src, act, own, order, order_side, raw, flags, buf, masks, stage, sems, out_sems):
    waits = fetch(jac, face, src, act, raw, flags, sems, BLOCK)
    order[...] = own_order()
    order_side[...] = side_order()
    outs = []
    for b, wait in enumerate(waits):
        wait()
        cols = slice(b * BLOCK, b * BLOCK + BLOCK)
        x = reorder(raw[:, cols], order[...])
        m = jnp.dot(flags[:, cols].astype(F32).astype(BF16), order[...], preferred_element_type=F32)
        for p in range(PHASES):
            buf[b % 2, p] = x[:, p * T : p * T + T]
            masks[b % 2, p] = m[:, p * T : p * T + T]
        if b >= 2:
            outs[b - 2].wait()
        place(buf.at[b % 2], masks.at[b % 2], stage.at[b % 2], slice(0, T), None)
        outs.append(pltpu.make_async_copy(stage.at[b % 2], own.at[:, :, :, :, pl.ds(b * T, T)], out_sems.at[b]))
        outs[b].start()
    for copy in outs[-2:]:
        copy.wait()


def row_flag(ends, r):
    if r < WIDE:
        return ends[0]
    if r >= WIDE + ROWS:
        return ends[1]
    return None


def merge(fine):
    count = len(fine[0]) // 2
    sub = iota(fine[0][0].shape, 0)
    f0, f1, f2, f3 = fine[FIELDS : FIELDS + 4]
    inner = [f1[2 * p + 1] + f0[2 * p] for p in range(count)]
    coarse = []
    for f in range(FIELDS):
        both = [fine[f][2 * p] + fine[f][2 * p + 1] for p in range(count)]
        coarse.append([jnp.where(sub == f, both[p] - inner[p], both[p]) for p in range(count)])
    coarse.append([f0[2 * p + 1] for p in range(count)])
    coarse.append([f1[2 * p] for p in range(count)])
    coarse.append([f2[2 * p] + f2[2 * p + 1] for p in range(count)])
    coarse.append([f3[2 * p] + f3[2 * p + 1] for p in range(count)])
    return coarse


def build_levels(read, outs, sl, domain):
    fine = [[read(k, p) for p in range(PHASES)] for k in range(PLANES - 1)]
    for write in outs:
        fine = merge(fine)
        for p in range(len(fine[0])):
            weight = DAMP / diagonal([fine[f][p] for f in range(FIELDS)])
            if domain is not None:
                weight = jnp.where(domain > 0.0, weight, 0.0)
            if write is not None:
                for k, planes in enumerate(fine):
                    write(k, p, planes[p])
                write(SWEEP_W, p, weight)


def levels_kernel(ends, main, near, c1, c2):
    tiles = main.shape[-1] // T
    sides = side_domain(ends)

    def build(source, row, r, sl, domain):
        def put(out):
            def write(k, p, x):
                out[r, k, p, :, sl] = x

            return write

        build_levels(lambda k, p: source[row, k, p, :, sl], [put(c1), put(c2)], sl, domain)

    def body(r):
        each(tiles - 1, lambda j: build(main, r, r + WIDE, tile(j), None))

    each(ROWS, body)
    sl = slice((tiles - 1) * T, tiles * T)
    each(ROWS, lambda r: build(main, r, r + WIDE, sl, sides))
    for i, r in enumerate((1, EXT - 2)):
        each(tiles - 1, lambda j: build(near, i, r, tile(j), row_flag(ends, r)))
        build(near, i, r, sl, sides * row_flag(ends, r))


def far_kernel(ends, rows_above, rows_below, corner_above, corner_below, order, order_side, far, order_out):
    order_out[...] = natural_order()
    wide = far.shape[-1]

    def put(i, p, planes, mask, sl):
        faces = planes[FIELDS : FIELDS + 4]
        jac = with_face_sum(planes[:FIELDS], faces)
        for k, x in enumerate(jac + faces + [weight_of(jac, mask), planes[PLANES - 1]]):
            far[i, k, p, :, sl] = x

    def fill(j):
        cols = pl.ds(pl.multiple_of(j * BLOCK, BLOCK), BLOCK)
        for i, rows in enumerate((rows_above, rows_below)):
            x = reorder(rows[FINE : FINE + PLANES, :, cols].reshape(PLANES * 8, BLOCK), order[...])
            for p in range(PHASES):
                planes = [x[k * 8 : k * 8 + 8, p * T : p * T + T] for k in range(PLANES)]
                put(i, p, planes, planes[PLANES - 1][FIELDS : FIELDS + 1] * ends[i], tile(j))

    each(wide // T - 1, fill)
    corners = corner_planes((corner_above, corner_below), order_side[...])
    for i in range(2):
        domain = side_domain(ends) * ends[i]
        planes, masks = corners[2 * i + 1]
        for p in range(PHASES):
            put(i, p, [x[p] for x in planes], jnp.where(domain > 0.0, masks[p], 0.0), slice(wide - T, wide))


def apply_at(c, r, v, j, above=None, below=None):
    tiles = c.shape[-1] // T
    count = c.shape[2]
    sl = tile(j)
    before = tile(lax.rem(j + tiles - 1, tiles))
    after = tile(lax.rem(j + 1, tiles))
    lane = iota((8, T), 1)
    here = [v[r, p, :, sl] for p in range(count)]
    k = FIELDS
    east = [c[r, k, p, :, sl] * here[p] for p in range(count)]
    west = [c[r, k + 1, p, :, sl] * here[p] for p in range(count)]
    end = count - 1
    wrap = jnp.where(lane == T - 1, c[r, k, end, :, before] * v[r, end, :, before], east[end])
    from_left = [pltpu.roll(wrap, 1, 1)] + east[:end]
    wrap = jnp.where(lane == 0, c[r, k + 1, 0, :, after] * v[r, 0, :, after], west[0])
    from_right = west[1:] + [pltpu.roll(wrap, T - 1, 1)]
    outs = []
    for p in range(count):
        out = c[r, 0, p, :, sl] * v[r, p, 0:1, sl]
        for f in range(1, FIELDS):
            out = out + c[r, f, p, :, sl] * v[r, p, f : f + 1, sl]
        up = c[r - 1, k + 2, p, :, sl] * v[r - 1, p, :, sl] if above is None else above[p, :, sl]
        down = c[r + 1, k + 3, p, :, sl] * v[r + 1, p, :, sl] if below is None else below[p, :, sl]
        outs.append(out - (from_left[p] + from_right[p]) - (up + down))
    return outs


def smooth(c, t, old, new, first, last, above=None, below=None):
    def body(j):
        sl = tile(j)
        for r in range(first, last):
            up = above if r == first else None
            down = below if r == last - 1 else None
            for p, out in enumerate(apply_at(c, r, old, j, up, down)):
                diff = t[r, p, :, sl] - out
                new[r, p, :, sl] = old[r, p, :, sl] + diff * c[r, SWEEP_W, p, :, sl]

    each(c.shape[-1] // T, body)


def gather_rows(out, own, above, below, j, wide, weight=None):
    sl = tile(j)
    for r in range(WIDE - wide, WIDE + ROWS + wide):
        for p in range(out.shape[1]):
            if r < WIDE:
                val = above[WIDE - 1 - r, p, :, sl]
            elif r < WIDE + ROWS:
                val = own[r - WIDE, p, :, sl]
            else:
                val = below[r - WIDE - ROWS, p, :, sl]
            if weight is not None and not WIDE <= r < WIDE + ROWS:
                val = jnp.where(weight[r, SWEEP_W, p, :, sl] != 0.0, val, 0.0)
            out[r, p, :, sl] = val


def send_rows(top, bottom, row, p, sl, val, wide, product):
    if row < wide:
        top[row, p, :, sl] = val
    if row >= ROWS - wide:
        bottom[ROWS - 1 - row, p, :, sl] = val
    if row == wide:
        top[wide, p, :, sl] = product(FIELDS + 3)
    if row == ROWS - 1 - wide:
        bottom[wide, p, :, sl] = product(FIELDS + 2)


def first_kernel(ends, main, rows_above, rows_below, corner_above, corner_below, order, order_side, near, v2, t1, t1_top, t1_bottom, sums, va, vb, prods):
    tiles = main.shape[-1] // T
    c0 = FineRows(main, near)
    t0 = SourceOf(c0)
    last = slice((tiles - 1) * T, tiles * T)

    def put(i, p, planes, mask, sl):
        faces = planes[FIELDS : FIELDS + 4]
        source = planes[PLANES - 1]
        jac = with_face_sum(planes[:FIELDS], faces)
        weight = weight_of(jac, mask)
        for k, x in enumerate(jac + faces + [weight, source]):
            near[i, k, p, :, sl] = x
        va[1 if i == 0 else EXT - 2, p, :, sl] = weight * source

    def fill(j):
        sl = tile(j)
        cols = pl.ds(pl.multiple_of(j * BLOCK, BLOCK), BLOCK)
        for i, rows in enumerate((rows_above, rows_below)):
            x = reorder(rows[0:FINE, :, cols].reshape(FINE * 8, BLOCK), order[...])
            for p in range(PHASES):
                planes = [x[k * 8 : k * 8 + 8, p * T : p * T + T] for k in range(FINE)]
                put(i, p, planes, planes[PLANES - 1][FIELDS : FIELDS + 1] * ends[i], sl)
                prods[i, p, :, sl] = planes[PLANES]

    each(tiles - 1, fill)
    sides = side_domain(ends)
    corners = corner_planes((corner_above, corner_below), order_side[...])
    for i in range(2):
        domain = sides * ends[i]
        planes, masks = corners[2 * i]
        far, far_masks = corners[2 * i + 1]
        for p in range(PHASES):
            put(i, p, [x[p] for x in planes], jnp.where(domain > 0.0, masks[p], 0.0), last)
            here = [x[p] for x in far]
            jac = with_face_sum(here[:FIELDS], here[FIELDS : FIELDS + 4])
            weight = weight_of(jac, jnp.where(domain > 0.0, far_masks[p], 0.0))
            prods[i, p, :, last] = here[FIELDS + 2 + i] * weight * here[PLANES - 1]

    def own(j):
        sl = tile(j)
        for r in range(WIDE, WIDE + ROWS):
            for p in range(PHASES):
                va[r, p, :, sl] = c0[r, SWEEP_W, p, :, sl] * t0[r, p, :, sl]

    each(tiles, own)

    smooth(c0, t0, va, vb, 1, EXT - 1, prods.at[0], prods.at[1])
    sums[...] = jnp.zeros_like(sums)

    def rest(j):
        sl = tile(j)
        total = jnp.zeros((8, T), F32)
        for r in range(WIDE, WIDE + ROWS):
            res = []
            for p, out in enumerate(apply_at(c0, r, vb, j)):
                diff = t0[r, p, :, sl] - out
                res.append(jnp.where(c0[r, SWEEP_W, p, :, sl] != 0.0, diff, 0.0))
                total = total + res[p] * res[p]
                v2[r - WIDE, p, :, sl] = vb[r, p, :, sl]
            row = r - WIDE
            if row in (1, ROWS - 2):
                coarse = merge([[c0[r, k, p, :, sl] for p in range(PHASES)] for k in range(PLANES - 1)])
            for p in range(PHASES // 2):
                val = res[2 * p] + res[2 * p + 1]
                t1[row, p, :, sl] = val

                def product(k):
                    diag = diagonal([coarse[f][p] for f in range(FIELDS)])
                    return coarse[k][p] * jnp.where(diag > 0.0, DAMP / diag, 0.0) * val

                send_rows(t1_top, t1_bottom, row, p, sl, val, 1, product)
        sums[...] += jnp.where(j < tiles - 1, total, 0.0)

    each(tiles, rest)


def second_kernel(c1, c2, t1_own, above, below, t1, e1, t2, top, bottom, sums, va, vb):
    tiles = c1.shape[-1] // T

    def fill(j):
        sl = tile(j)
        gather_rows(t1, t1_own, above, below, j, 1)
        for r in range(1, EXT - 1):
            for p in range(2):
                va[r, p, :, sl] = c1[r, SWEEP_W, p, :, sl] * t1[r, p, :, sl]

    each(tiles, fill)
    smooth(c1, t1, va, vb, 1, EXT - 1, above.at[1], below.at[1])
    sums[...] = jnp.zeros_like(sums)

    def rest(j):
        sl = tile(j)
        total = jnp.zeros((8, T), F32)
        for r in range(WIDE, WIDE + ROWS):
            res = [t1[r, p, :, sl] - out for p, out in enumerate(apply_at(c1, r, vb, j))]
            total = total + res[0] * res[0] + res[1] * res[1]
            for p in range(2):
                e1[r - WIDE, p, :, sl] = vb[r, p, :, sl]
            val = res[0] + res[1]
            t2[r - WIDE, 0, :, sl] = val

            def product(k):
                return c2[r, k, 0, :, sl] * c2[r, SWEEP_W, 0, :, sl] * val

            send_rows(top, bottom, r - WIDE, 0, sl, val, WIDE, product)
        sums[...] += jnp.where(j < tiles - 1, total, 0.0)

    each(tiles, rest)


def third_kernel(ends, main, c1, far0, t2_own, above, below, e1_in, e1, top, bottom, t2, va, vb, far):
    tiles = main.shape[-1] // T
    sides = side_domain(ends)

    def build(i, sl, domain):
        def write(k, p, x):
            far[i, k, p, :, sl] = x

        build_levels(lambda k, p: far0[i, k, p, :, sl], [None, write], sl, domain)

    for i in range(2):
        each(tiles - 1, lambda j: build(i, tile(j), ends[i]))
        build(i, slice((tiles - 1) * T, tiles * T), sides * ends[i])
    c2 = WithFar(main, far)

    def fill(j):
        sl = tile(j)
        gather_rows(t2, t2_own, above, below, j, WIDE)
        for r in range(EXT):
            va[r, 0, :, sl] = c2[r, SWEEP_W, 0, :, sl] * t2[r, 0, :, sl]

    each(tiles, fill)
    smooth(c2, t2, va, vb, 0, EXT, above.at[WIDE], below.at[WIDE])
    smooth(c2, t2, vb, va, 1, EXT - 1)
    smooth(c2, t2, va, vb, WIDE, WIDE + ROWS)

    def last(j):
        sl = tile(j)
        for r in range(WIDE, WIDE + ROWS):
            for p in range(2):
                val = e1_in[r - WIDE, p, :, sl] + vb[r, 0, :, sl]
                e1[r - WIDE, p, :, sl] = val
                send_rows(top, bottom, r - WIDE, p, sl, val, 1, lambda k: c1[r, k, p, :, sl] * val)

    each(tiles, last)


def fourth_kernel(c1, main, t1, e1, above, below, v2, v, top, bottom, va, vb):
    tiles = c1.shape[-1] // T
    each(tiles, lambda j: gather_rows(va, e1, above, below, j, 1, c1))
    smooth(c1, t1, va, vb, 1, EXT - 1, above.at[1], below.at[1])
    smooth(c1, t1, vb, va, WIDE, WIDE + ROWS)

    def last(j):
        sl = tile(j)
        for r in range(ROWS):
            for p in range(PHASES):
                add = jnp.where(main[r, SWEEP_W, p, :, sl] != 0.0, va[r + WIDE, p // 2, :, sl], 0.0)
                val = v2[r, p, :, sl] + add
                v[r, p, :, sl] = val
                send_rows(top, bottom, r, p, sl, val, WIDE, lambda k: main[r, k, p, :, sl] * val)

    each(tiles, last)


def fifth_kernel(main, near, far, v, above, below, order, adjoint, residual, sums, va, vb, buf):
    tiles = main.shape[-1] // T
    c0 = FineRows(main, near, far)
    t0 = SourceOf(c0)
    each(tiles, lambda j: gather_rows(va, v, above, below, j, WIDE, c0))
    smooth(c0, t0, va, vb, 0, EXT, above.at[WIDE], below.at[WIDE])
    smooth(c0, t0, vb, va, 1, EXT - 1)
    sums[...] = jnp.zeros_like(sums)

    def rest(j):
        sl = tile(j)
        total = jnp.zeros((8, T), F32)
        for r in range(WIDE, WIDE + ROWS):
            for p, out in enumerate(apply_at(c0, r, va, j)):
                diff = t0[r, p, :, sl] - out
                res = jnp.where(c0[r, SWEEP_W, p, :, sl] != 0.0, diff, 0.0)
                total = total + res * res
                buf[p, pl.ds(r - WIDE, FIELDS, stride=ROWS), :] = va[r, p, 0:FIELDS, sl]
                buf[p, pl.ds(GRID + r - WIDE, FIELDS, stride=ROWS), :] = res[0:FIELDS]
        sums[...] += total
        x = jnp.concatenate([buf[p] for p in range(PHASES)], axis=1)
        y = reorder(x, order[...])
        cols = pl.ds(pl.multiple_of(j * BLOCK, BLOCK), BLOCK)
        adjoint[:, cols] = y[0:GRID]
        residual[:, cols] = y[GRID : 2 * GRID]

    each(tiles - 1, rest)


def call(kernel, outs, args, scratch=(), spaces=None, size=0, limit=LIMIT, out_spaces=None):
    spaces = spaces or {}
    return pl.pallas_call(
        kernel,
        out_shape=[jax.ShapeDtypeStruct(s, F32) if isinstance(s, tuple) else s for s in outs],
        in_specs=[pl.BlockSpec(memory_space=spaces.get(i, pltpu.VMEM)) for i in range(len(args))],
        out_specs=[pl.BlockSpec(memory_space=(out_spaces or {}).get(i, pltpu.VMEM)) for i in range(len(outs))],
        scratch_shapes=[pltpu.VMEM(s, F32) if isinstance(s, tuple) else s for s in scratch],
        compiler_params=pltpu.CompilerParams(vmem_limit_bytes=limit),
        cost_estimate=pl.CostEstimate(flops=0, bytes_accessed=size, transcendentals=0),
        name=kernel.__name__,
    )(*args)


def ring(x, axis, step):
    count = lax.axis_size(axis)
    return lax.ppermute(x, axis, [(i, (i + step) % count) for i in range(count)])


def total_over_devices(x):
    axes = ("hull", "blk")
    count = lax.axis_size(axes)
    sent = jnp.broadcast_to(jnp.pad(x, (0, T - x.size))[None], (count, T))
    return jnp.sum(lax.all_to_all(sent, axes, 0, 0, tiled=True), axis=0)[: x.size]


def on_device(source, jacobian, face_coef, active):
    columns = source.shape[2]
    quads = columns // PHASES
    wide = quads + T
    blocks = columns // BLOCK
    hull, blk = lax.axis_index("hull"), lax.axis_index("blk")
    ends = jnp.stack([hull > 0, hull < lax.axis_size("hull") - 1, blk > 0, blk < lax.axis_size("blk") - 1]).astype(F32)

    def cells(rows, phases):
        return (rows, phases, 8, wide)

    def coefs(rows, planes, phases):
        return (rows, planes, phases, 8, wide)

    flag = {0: pltpu.SMEM}
    inputs = [
        pltpu.with_memory_space_constraint(x, pltpu.HBM)
        for x in (
            jacobian.reshape(FIELDS, GRID, columns),
            face_coef.reshape(4, GRID, columns),
            source.reshape(GRID, columns),
            active,
        )
    ]
    in_hbm = {i: pltpu.HBM for i in range(len(inputs))}
    staged = [(RAW, columns), pltpu.VMEM((ROWS, columns), jnp.int32)]
    copies = pltpu.SemaphoreType.DMA((blocks, PLANES + 1))
    order = jax.ShapeDtypeStruct((BLOCK, BLOCK), BF16)
    order_side = jax.ShapeDtypeStruct((2 * T, BLOCK), BF16)
    sum_tile = (8, T)

    top, bottom, left, right = call(
        send_kernel,
        [(FINE + PLANES, 8, columns)] * 2 + [(PACK + ROWS, T)] * 2,
        inputs,
        [*staged, (RAW, T), copies],
        in_hbm,
        limit=12 * 2**20,
    )
    from_right = ring(left, "blk", -1)
    from_left = ring(right, "blk", 1)
    rows_below = ring(top, "hull", -1)
    rows_above = ring(bottom, "hull", 1)
    inner, own, side = call(
        own_kernel,
        [pltpu.HBM((ROWS, FINE, PHASES, 8, quads), F32), order, order_side],
        inputs,
        [
            *staged,
            (2, PHASES, RAW, T),
            (2, PHASES, ROWS, T),
            (2, ROWS, FINE, PHASES, 8, T),
            copies,
            pltpu.SemaphoreType.DMA((blocks,)),
        ],
        in_hbm,
        size=25 * 10**6,
        limit=16 * 2**20,
        out_spaces={0: pltpu.HBM},
    )
    inner = pltpu.with_memory_space_constraint(inner, pltpu.HBM)
    corner = (2, 2, PER_GROUP * 8, T)
    top, bottom = call(corner_kernel, [corner, corner], [from_right, from_left, side], spaces={2: pl.ANY})
    corner_below = ring(top, "hull", -1)
    corner_above = ring(bottom, "hull", 1)
    (main,) = call(
        side_kernel,
        [coefs(ROWS, FINE, 4)],
        [ends, from_right, from_left, inner, side],
        [(PHASES, RAW, T), (PHASES, ROWS, T), pltpu.SemaphoreType.DMA((ROWS,))],
        {0: pltpu.SMEM, 3: pltpu.HBM},
        size=9 * 10**6,
    )
    near, v2, t1, top, bottom, sum0 = call(
        first_kernel,
        [coefs(2, FINE, 4), cells(ROWS, 4), cells(ROWS, 2), cells(2, 2), cells(2, 2), sum_tile],
        [ends, main, rows_above, rows_below, corner_above, corner_below, own, side],
        [cells(EXT, 4), cells(EXT, 4), cells(2, 4)],
        flag,
    )
    below = ring(top, "hull", -1)
    above = ring(bottom, "hull", 1)
    far, natural = call(
        far_kernel,
        [coefs(2, FINE, 4), order],
        [ends, rows_above, rows_below, corner_above, corner_below, own, side],
        (),
        flag,
        size=8 * 10**6,
    )
    c1, c2 = call(levels_kernel, [coefs(EXT, PLANES, 2), coefs(EXT, PLANES, 1)], [ends, main, near], (), flag, size=10**7)
    t1, e1, t2, top, bottom, sum1 = call(
        second_kernel,
        [cells(EXT, 2), cells(ROWS, 2), cells(ROWS, 1), cells(3, 1), cells(3, 1), sum_tile],
        [c1, c2, t1, above, below],
        [cells(EXT, 2)] * 2,
    )
    below = ring(top, "hull", -1)
    above = ring(bottom, "hull", 1)
    e1, top, bottom = call(
        third_kernel,
        [cells(ROWS, 2), cells(2, 2), cells(2, 2)],
        [ends, c2, c1, far, t2, above, below, e1],
        [cells(EXT, 1)] * 3 + [coefs(2, PLANES, 1)],
        flag,
    )
    below = ring(top, "hull", -1)
    above = ring(bottom, "hull", 1)
    v, top, bottom = call(
        fourth_kernel, [cells(ROWS, 4), cells(3, 4), cells(3, 4)], [c1, main, t1, e1, above, below, v2], [cells(EXT, 2)] * 2
    )
    below = ring(top, "hull", -1)
    above = ring(bottom, "hull", 1)
    adjoint, residual, sum2 = call(
        fifth_kernel,
        [(GRID, columns), (GRID, columns), sum_tile],
        [main, near, far, v, above, below, natural],
        [cells(EXT, 4)] * 2 + [(PHASES, 2 * GRID, T)],
    )
    squares = jnp.stack([sum0, 2.0 * sum1, sum2])
    squares = total_over_devices(jnp.sum(squares[:, :FIELDS], axis=(1, 2)))
    count = source.size * lax.axis_size("hull") * lax.axis_size("blk")
    level_rms = jnp.sqrt(squares / float(count))
    return adjoint.reshape(source.shape), residual.reshape(source.shape), level_rms


def solution(mesh):
    return jax.shard_map(
        on_device,
        mesh=mesh,
        in_specs=(
            P(None, "hull", "blk"),
            P(None, None, "hull", "blk"),
            P(None, None, "hull", "blk"),
            P("hull", "blk"),
        ),
        out_specs=(P(None, "hull", "blk"), P(None, "hull", "blk"), P()),
        check_vma=False,
    )
```

```python
import jax
import jax.numpy as jnp
from jax import lax
from jax.experimental import pallas as pl
from jax.experimental.pallas import tpu as pltpu
from jax.sharding import PartitionSpec as P

FIELDS = 7
ROWS = 8
WIDE = 2
EXT = ROWS + 2 * WIDE
T = 128
PHASES = 4
BLOCK = PHASES * T
SIDE = 8
SIDE_COLS = SIDE * PHASES
DAMP = 0.7
PLANES = 12
SWEEP_W = 11
SOURCE = 12
FINE = 13
SENT = 22
F32 = jnp.float32
BF16 = jnp.bfloat16
LIMIT = 12 * 2**20
GRID = FIELDS * ROWS
RAW = PLANES * GRID
GROUPS = T // SIDE_COLS
PACK = RAW // GROUPS
PER_GROUP = PLANES // GROUPS


def iota(shape, dim):
    return lax.broadcasted_iota(jnp.int32, shape, dim)


def tile(j):
    return pl.ds(pl.multiple_of(j * T, T), T)


def each(count, body):
    def step(j, carry):
        body(j)
        return carry

    lax.fori_loop(0, count, step, 0)


class FineRows:
    def __init__(self, main, near, far=None):
        self.main, self.near, self.far = main, near, far
        self.shape = main.shape

    def __getitem__(self, at):
        r, *rest = at
        if r in (0, EXT - 1):
            return self.far[(r // (EXT - 1), *rest)]
        if r in (1, EXT - 2):
            return self.near[(r // (EXT - 2), *rest)]
        return self.main[(r - WIDE, *rest)]


class WithFar:
    def __init__(self, main, far):
        self.main, self.far = main, far
        self.shape = main.shape

    def __getitem__(self, at):
        r, *rest = at
        if r in (0, EXT - 1):
            return self.far[(r // (EXT - 1), *rest)]
        return self.main[(r, *rest)]


class SourceOf:
    def __init__(self, c):
        self.c = c

    def __getitem__(self, at):
        r, *rest = at
        return self.c[(r, SOURCE, *rest)]


def own_order():
    rows, cols = iota((BLOCK, BLOCK), 0), iota((BLOCK, BLOCK), 1)
    return jnp.where(rows == (cols % T) * PHASES + cols // T, 1.0, 0.0).astype(BF16)


def natural_order():
    rows, cols = iota((BLOCK, BLOCK), 0), iota((BLOCK, BLOCK), 1)
    return jnp.where(cols == (rows % T) * PHASES + rows // T, 1.0, 0.0).astype(BF16)


def side_order():
    rows, cols = iota((2 * T, BLOCK), 0), iota((2 * T, BLOCK), 1)
    lane, phase = cols % T, cols // T
    at = rows % SIDE_COLS
    after = (lane < SIDE) & (rows < T) & (at == lane * PHASES + phase)
    before = (lane >= T - SIDE) & (rows >= T) & (at == (lane - T + SIDE) * PHASES + phase)
    return jnp.where(after | before, 1.0, 0.0).astype(BF16)


def group_of(x, g):
    return jnp.where(iota(x.shape, 1) % T // SIDE_COLS == g, x, 0.0)


def reorder(x, order):
    high = x.astype(BF16)
    low = (x - high.astype(F32)).astype(BF16)
    return jnp.dot(high, order, preferred_element_type=F32) + jnp.dot(low, order, preferred_element_type=F32)


def diagonal(planes):
    sub = iota(planes[0].shape, 0)
    out = planes[FIELDS - 1]
    for f in range(FIELDS - 1):
        out = jnp.where(sub == f, planes[f], out)
    return out


def with_face_sum(planes, faces):
    total = faces[0] + faces[1] + faces[2] + faces[3]
    sub = iota(total.shape, 0)
    return [jnp.where(sub == f, x + total, x) for f, x in enumerate(planes)]


def last_sublanes(planes):
    sub = iota(planes[0].shape, 0)
    out = planes[FIELDS - 1][FIELDS:8]
    for f in range(FIELDS - 1):
        out = jnp.where(sub == f, planes[f][FIELDS:8], out)
    return out


def weight_of(planes, mask):
    return jnp.where(mask > 0.0, DAMP / diagonal(planes), 0.0)


def fetch(jac, face, src, act, raw, flags, sems, columns):
    blocks = src.shape[-1] // columns

    def copies(b):
        cols = pl.ds(b * columns, columns)
        moves = [(jac.at[f, :, cols], raw.at[pl.ds(f * GRID, GRID), cols]) for f in range(FIELDS)]
        moves += [(face.at[k, :, cols], raw.at[pl.ds((FIELDS + k) * GRID, GRID), cols]) for k in range(4)]
        moves += [(src.at[:, cols], raw.at[pl.ds((PLANES - 1) * GRID, GRID), cols])]
        moves += [(act.at[:, cols], flags.at[:, cols])]
        return [pltpu.make_async_copy(a, d, sems.at[b, i]) for i, (a, d) in enumerate(moves)]

    todo = [copies(b) for b in range(blocks)]
    for group in todo:
        for copy in group:
            copy.start()

    def waiter(group):
        def wait():
            for copy in group:
                copy.wait()

        return wait

    return [waiter(group) for group in todo]


def send_kernel(jac, face, src, act, top, bottom, left, right, raw, flags, buf, stage, sems, out_sems):
    columns = src.shape[-1]
    waits = fetch(jac, face, src, act, raw, flags, sems, BLOCK)
    per = BLOCK // T
    jobs = ((0, 0, 1, 3), (1, ROWS - 1, ROWS - 2, 2))

    def rows_of(b):
        def body(i):
            sl = tile(b * per + i)
            for k in range(PLANES):
                buf[k * GRID : k * GRID + GRID] = raw[k * GRID : k * GRID + GRID, sl]

            def row(r):
                planes = [buf[pl.ds(k * GRID + r, FIELDS, stride=ROWS), :] for k in range(PLANES)]
                faces = planes[FIELDS : FIELDS + 4]
                return with_face_sum(planes[:FIELDS], faces), faces, planes[PLANES - 1], flags[r : r + 1, sl].astype(F32)

            for out, near, far, face_k in jobs:
                planes, faces, source, mask = row(near)
                for k, x in enumerate(planes + faces + [source]):
                    stage[out, k, 0:FIELDS, sl] = x
                stage[out, PLANES - 1, FIELDS:8, sl] = mask
                planes, faces, source, mask = row(far)
                product = faces[face_k] * weight_of(planes, mask) * source
                for k, x in enumerate(planes + [faces[0], faces[1], faces[face_k]]):
                    stage[out, PLANES + k, 0:FIELDS, sl] = x
                for g in range(FIELDS):
                    stage[out, g, FIELDS:8, sl] = product[g : g + 1]
                    stage[out, PLANES + g, FIELDS:8, sl] = source[g : g + 1]
                stage[out, PLANES + FIELDS, FIELDS:8, sl] = mask

        each(per, body)

    copies = []
    for b, wait in enumerate(waits):
        wait()
        rows_of(b)
        cols = pl.ds(b * BLOCK, BLOCK)
        for i, out in enumerate((top, bottom)):
            copies.append(pltpu.make_async_copy(stage.at[i, :, :, cols], out.at[:, :, cols], out_sems.at[b, i]))
            copies[-1].start()
    lane = iota((PACK, T), 1) // SIDE_COLS
    for out, at, move in ((left, 0, 0), (right, columns - T, SIDE_COLS)):
        packed = None
        for g in range(GROUPS):
            part = raw[g * PACK : g * PACK + PACK, at : at + T]
            shift = (g * SIDE_COLS + move) % T
            part = pltpu.roll(part, shift, 1) if shift else part
            packed = part if packed is None else jnp.where(lane == g, part, packed)
        out[0:PACK] = packed
        mask = flags[:, at : at + T].astype(F32)
        out[PACK : PACK + ROWS] = pltpu.roll(mask, move, 1) if move else mask
    for copy in copies:
        copy.wait()


def place(buf, masks, out, sl, domain):
    for r in range(ROWS):
        for p in range(PHASES):
            def pick(k):
                return buf[p, pl.ds(k * GRID + r, FIELDS, stride=ROWS), :]

            faces = [pick(FIELDS + k) for k in range(4)]
            planes = with_face_sum([pick(f) for f in range(FIELDS)], faces)
            mask = masks[p, r : r + 1, :]
            if domain is not None:
                mask = jnp.where(domain > 0.0, mask, 0.0)
            for k, x in enumerate(planes + faces + [weight_of(planes, mask), pick(PLANES - 1)]):
                out[r, k, p, 0:FIELDS, sl] = x


def side_domain(ends):
    lane = iota((1, T), 1)
    return jnp.where(lane < SIDE, ends[3], jnp.where(lane >= T - SIDE, ends[2], 0.0))


def corner_kernel(from_right, from_left, token, top, bottom):
    for side, packed in enumerate((from_right, from_left)):
        for out, rows in ((top, (0, 1)), (bottom, (ROWS - 1, ROWS - 2))):
            for i, r in enumerate(rows):
                for k in range(PER_GROUP):
                    out[i, side, k * 8 : k * 8 + FIELDS] = packed[pl.ds(k * GRID + r, FIELDS, stride=ROWS), :]
                out[i, side, FIELDS : FIELDS + 1] = packed[PACK + r : PACK + r + 1]


def corner_planes(corners, order):
    parts = [jnp.concatenate([c[i, 0], c[i, 1]], axis=1) for c in corners for i in range(2)]
    both = jnp.concatenate(parts, axis=0)
    size = PER_GROUP * 8
    every = reorder(jnp.concatenate([group_of(both, g) for g in range(GROUPS)], axis=0), order)
    packs = [every[g * both.shape[0] : (g + 1) * both.shape[0]] for g in range(GROUPS)]
    result = []
    for n in range(len(parts)):
        def plane(k, p):
            first = n * size + k % PER_GROUP * 8
            return packs[k // PER_GROUP][first : first + 8, p * T : p * T + T]

        planes = [[plane(k, p) for p in range(PHASES)] for k in range(PLANES)]
        masks = [planes[0][p][FIELDS : FIELDS + 1] for p in range(PHASES)]
        result.append((planes, masks))
    return result


def side_kernel(ends, from_right, from_left, own, main, order_own, order, buf, masks, sems):
    inner = own.shape[-1]
    copies = [pltpu.make_async_copy(own.at[r], main.at[r, :, :, :, pl.ds(0, inner)], sems.at[r]) for r in range(ROWS)]
    for copy in copies:
        copy.start()
    order[...] = side_order()
    order_own[...] = own_order()
    both = jnp.concatenate([from_right[...], from_left[...]], axis=1)
    every = reorder(jnp.concatenate([group_of(both, g) for g in range(GROUPS)], axis=0), order[...])
    for g in range(GROUPS):
        x = every[g * (PACK + ROWS) : (g + 1) * (PACK + ROWS)]
        for p in range(PHASES):
            buf[p, g * PACK : g * PACK + PACK] = x[0:PACK, p * T : p * T + T]
            if g == 0:
                masks[p] = x[PACK : PACK + ROWS, p * T : p * T + T]
    place(buf, masks, main, slice(inner, inner + T), side_domain(ends))
    for copy in copies:
        copy.wait()


def own_kernel(jac, face, src, act, own, token, order, buf, masks, stage, out_sems):
    order[...] = own_order()
    token[...] = jnp.zeros_like(token)
    outs = []
    for b in range(src.shape[-1] // BLOCK):
        cols = slice(b * BLOCK, b * BLOCK + BLOCK)
        parts = [jac[f, :, cols] for f in range(FIELDS)] + [face[k, :, cols] for k in range(4)] + [src[:, cols]]
        x = reorder(jnp.concatenate(parts, axis=0), order[...])
        m = jnp.dot(act[:, cols].astype(F32).astype(BF16), order[...], preferred_element_type=F32)
        for p in range(PHASES):
            buf[b % 2, p] = x[:, p * T : p * T + T]
            masks[b % 2, p] = m[:, p * T : p * T + T]
        if b >= 2:
            outs[b - 2].wait()
        place(buf.at[b % 2], masks.at[b % 2], stage.at[b % 2], slice(0, T), None)
        outs.append(pltpu.make_async_copy(stage.at[b % 2], own.at[:, :, :, :, pl.ds(b * T, T)], out_sems.at[b]))
        outs[b].start()
    for copy in outs[-2:]:
        copy.wait()


def row_flag(ends, r):
    if r < WIDE:
        return ends[0]
    if r >= WIDE + ROWS:
        return ends[1]
    return None


def merge(fine):
    count = len(fine[0]) // 2
    sub = iota(fine[0][0].shape, 0)
    f0, f1, f2, f3 = fine[FIELDS : FIELDS + 4]
    inner = [f1[2 * p + 1] + f0[2 * p] for p in range(count)]
    coarse = []
    for f in range(FIELDS):
        both = [fine[f][2 * p] + fine[f][2 * p + 1] for p in range(count)]
        coarse.append([jnp.where(sub == f, both[p] - inner[p], both[p]) for p in range(count)])
    coarse.append([f0[2 * p + 1] for p in range(count)])
    coarse.append([f1[2 * p] for p in range(count)])
    coarse.append([f2[2 * p] + f2[2 * p + 1] for p in range(count)])
    coarse.append([f3[2 * p] + f3[2 * p + 1] for p in range(count)])
    return coarse


def build_levels(read, outs, sl, domain):
    fine = [[read(k, p) for p in range(PHASES)] for k in range(PLANES - 1)]
    for write in outs:
        fine = merge(fine)
        for p in range(len(fine[0])):
            weight = DAMP / diagonal([fine[f][p] for f in range(FIELDS)])
            if domain is not None:
                weight = jnp.where(domain > 0.0, weight, 0.0)
            if write is not None:
                for k, planes in enumerate(fine):
                    write(k, p, planes[p])
                write(SWEEP_W, p, weight)


def levels_kernel(ends, main, near, c1, c2):
    tiles = main.shape[-1] // T
    sides = side_domain(ends)

    def build(source, row, r, sl, domain):
        def put(out):
            def write(k, p, x):
                out[r, k, p, :, sl] = x

            return write

        build_levels(lambda k, p: source[row, k, p, :, sl], [put(c1), put(c2)], sl, domain)

    def body(r):
        each(tiles - 1, lambda j: build(main, r, r + WIDE, tile(j), None))

    each(ROWS, body)
    sl = slice((tiles - 1) * T, tiles * T)
    each(ROWS, lambda r: build(main, r, r + WIDE, sl, sides))
    for i, r in enumerate((1, EXT - 2)):
        each(tiles - 1, lambda j: build(near, i, r, tile(j), row_flag(ends, r)))
        build(near, i, r, sl, sides * row_flag(ends, r))


def far_planes(ends, rows, corners, wide, put):
    def fill(j):
        for i in range(2):
            cells = []
            for p in range(PHASES):
                planes = [rows[i, j, k * 8 : k * 8 + 8, p * T : p * T + T] for k in range(SENT - PLANES)]
                mask = planes[FIELDS][FIELDS:8] * ends[i]
                cells.append((planes[:FIELDS], planes[FIELDS:], planes, mask))
            put(i, cells, tile(j), ends[i])

    each(wide // T - 1, fill)
    for i in range(2):
        domain = side_domain(ends) * ends[i]
        planes, masks = corners[2 * i + 1]
        cells = []
        for p in range(PHASES):
            raw = [x[p] for x in planes]
            faces = raw[FIELDS : FIELDS + 4]
            mask = jnp.where(domain > 0.0, masks[p], 0.0)
            cells.append((with_face_sum(raw[:FIELDS], faces), [faces[0], faces[1], faces[2 + i]], raw[PLANES - 1], mask))
        put(i, cells, slice(wide - T, wide), domain)


def far_kernel(ends, rows_above, rows_below, corner_above, corner_below, order, order_side, far, order_out, rows):
    order_out[...] = natural_order()
    reorder_rows(rows_above, rows_below, slice(PLANES, SENT), order[...], rows)

    def put(i, cells, sl, domain):
        for p, (planes, faces, source, mask) in enumerate(cells):
            for k, x in enumerate(planes + faces[:2]):
                far[i, k, p, :, sl] = x
            far[i, FIELDS + 2 + i, p, :, sl] = faces[2]
            far[i, SWEEP_W, p, :, sl] = weight_of(planes, mask)
            far[i, SOURCE, p, :, sl] = last_sublanes(source) if isinstance(source, list) else source

    corners = corner_planes((corner_above, corner_below), order_side[...])
    far_planes(ends, rows, corners, far.shape[-1], put)


def far_coarse_kernel(ends, rows_above, rows_below, corner_above, corner_below, order, order_side, far, rows):
    reorder_rows(rows_above, rows_below, slice(PLANES, SENT), order[...], rows)

    def put(i, cells, sl, domain):
        def read(k, p):
            planes, faces, _, _ = cells[p]
            return planes[k] if k < FIELDS else faces[min(k - FIELDS, 2)]

        def write(k, p, x):
            if k in (FIELDS + 2, FIELDS + 3) and k != FIELDS + 2 + i:
                return
            far[i, k, p, :, sl] = x

        build_levels(read, [None, write], sl, domain)

    corners = corner_planes((corner_above, corner_below), order_side[...])
    far_planes(ends, rows, corners, far.shape[-1], put)


def apply_at(c, r, v, j, above=None, below=None):
    tiles = c.shape[-1] // T
    count = c.shape[2]
    sl = tile(j)
    before = tile(lax.rem(j + tiles - 1, tiles))
    after = tile(lax.rem(j + 1, tiles))
    lane = iota((8, T), 1)
    here = [v[r, p, :, sl] for p in range(count)]
    k = FIELDS
    east = [c[r, k, p, :, sl] * here[p] for p in range(count)]
    west = [c[r, k + 1, p, :, sl] * here[p] for p in range(count)]
    end = count - 1
    wrap = jnp.where(lane == T - 1, c[r, k, end, :, before] * v[r, end, :, before], east[end])
    from_left = [pltpu.roll(wrap, 1, 1)] + east[:end]
    wrap = jnp.where(lane == 0, c[r, k + 1, 0, :, after] * v[r, 0, :, after], west[0])
    from_right = west[1:] + [pltpu.roll(wrap, T - 1, 1)]
    outs = []
    for p in range(count):
        out = c[r, 0, p, :, sl] * v[r, p, 0:1, sl]
        for f in range(1, FIELDS):
            out = out + c[r, f, p, :, sl] * v[r, p, f : f + 1, sl]
        up = c[r - 1, k + 2, p, :, sl] * v[r - 1, p, :, sl] if above is None else above[p, :, sl]
        down = c[r + 1, k + 3, p, :, sl] * v[r + 1, p, :, sl] if below is None else below[p, :, sl]
        outs.append(out - (from_left[p] + from_right[p]) - (up + down))
    return outs


def smooth(c, t, old, new, first, last, above=None, below=None):
    def body(j):
        sl = tile(j)
        for r in range(first, last):
            up = above if r == first else None
            down = below if r == last - 1 else None
            for p, out in enumerate(apply_at(c, r, old, j, up, down)):
                diff = t[r, p, :, sl] - out
                new[r, p, :, sl] = old[r, p, :, sl] + diff * c[r, SWEEP_W, p, :, sl]

    each(c.shape[-1] // T, body)


def gather_rows(out, own, above, below, j, wide, weight=None):
    sl = tile(j)
    for r in range(WIDE - wide, WIDE + ROWS + wide):
        for p in range(out.shape[1]):
            if r < WIDE:
                val = above[WIDE - 1 - r, p, :, sl]
            elif r < WIDE + ROWS:
                val = own[r - WIDE, p, :, sl]
            else:
                val = below[r - WIDE - ROWS, p, :, sl]
            if weight is not None and not WIDE <= r < WIDE + ROWS:
                val = jnp.where(weight[r, SWEEP_W, p, :, sl] != 0.0, val, 0.0)
            out[r, p, :, sl] = val


def send_rows(top, bottom, row, p, sl, val, wide, product):
    if row < wide:
        top[row, p, :, sl] = val
    if row >= ROWS - wide:
        bottom[ROWS - 1 - row, p, :, sl] = val
    if row == wide:
        top[wide, p, :, sl] = product(FIELDS + 3)
    if row == ROWS - 1 - wide:
        bottom[wide, p, :, sl] = product(FIELDS + 2)


def reorder_rows(rows_above, rows_below, planes, order, out):
    blocks = rows_above.shape[-1] // BLOCK
    size = (planes.stop - planes.start) * 8
    parts = [rows[planes, :, b * BLOCK : b * BLOCK + BLOCK].reshape(size, BLOCK) for rows in (rows_above, rows_below) for b in range(blocks)]
    x = reorder(jnp.concatenate(parts, axis=0), order)
    for n in range(len(parts)):
        out[n // blocks, n % blocks] = x[n * size : n * size + size]


def first_kernel(ends, main, rows_above, rows_below, corner_above, corner_below, order, order_side, near, v2, t1, t1_top, t1_bottom, sums, va, vb, prods, rows):
    tiles = main.shape[-1] // T
    c0 = FineRows(main, near)
    t0 = SourceOf(c0)
    last = slice((tiles - 1) * T, tiles * T)

    def put(i, p, planes, mask, sl):
        source = planes[PLANES - 1]
        weight = weight_of(planes[:FIELDS], mask)
        for k, x in enumerate(planes[: PLANES - 1] + [weight, source]):
            near[i, k, p, :, sl] = x
        va[1 if i == 0 else EXT - 2, p, :, sl] = weight * source

    def fill(j):
        sl = tile(j)
        for i in range(2):
            for p in range(PHASES):
                planes = [rows[i, j, k * 8 : k * 8 + 8, p * T : p * T + T] for k in range(PLANES)]
                put(i, p, planes, planes[PLANES - 1][FIELDS:8] * ends[i], sl)
                prods[i, p, :, sl] = last_sublanes(planes)

    reorder_rows(rows_above, rows_below, slice(0, PLANES), order[...], rows)
    each(tiles - 1, fill)
    sides = side_domain(ends)
    corners = corner_planes((corner_above, corner_below), order_side[...])
    for i in range(2):
        domain = sides * ends[i]
        planes, masks = corners[2 * i]
        far, far_masks = corners[2 * i + 1]
        for p in range(PHASES):
            raw = [x[p] for x in planes]
            raw[:FIELDS] = with_face_sum(raw[:FIELDS], raw[FIELDS : FIELDS + 4])
            put(i, p, raw, jnp.where(domain > 0.0, masks[p], 0.0), last)
            here = [x[p] for x in far]
            jac = with_face_sum(here[:FIELDS], here[FIELDS : FIELDS + 4])
            weight = weight_of(jac, jnp.where(domain > 0.0, far_masks[p], 0.0))
            prods[i, p, :, last] = here[FIELDS + 2 + i] * weight * here[PLANES - 1]

    def own(j):
        sl = tile(j)
        for r in range(WIDE, WIDE + ROWS):
            for p in range(PHASES):
                va[r, p, :, sl] = c0[r, SWEEP_W, p, :, sl] * t0[r, p, :, sl]

    each(tiles, own)

    smooth(c0, t0, va, vb, 1, EXT - 1, prods.at[0], prods.at[1])
    sums[...] = jnp.zeros_like(sums)

    def rest(j):
        sl = tile(j)
        total = jnp.zeros((8, T), F32)
        for r in range(WIDE, WIDE + ROWS):
            res = []
            for p, out in enumerate(apply_at(c0, r, vb, j)):
                diff = t0[r, p, :, sl] - out
                res.append(jnp.where(c0[r, SWEEP_W, p, :, sl] != 0.0, diff, 0.0))
                total = total + res[p] * res[p]
                v2[r - WIDE, p, :, sl] = vb[r, p, :, sl]
            row = r - WIDE
            if row in (1, ROWS - 2):
                coarse = merge([[c0[r, k, p, :, sl] for p in range(PHASES)] for k in range(PLANES - 1)])
            for p in range(PHASES // 2):
                val = res[2 * p] + res[2 * p + 1]
                t1[row, p, :, sl] = val

                def product(k):
                    diag = diagonal([coarse[f][p] for f in range(FIELDS)])
                    return coarse[k][p] * jnp.where(diag > 0.0, DAMP / diag, 0.0) * val

                send_rows(t1_top, t1_bottom, row, p, sl, val, 1, product)
        sums[...] += jnp.where(j < tiles - 1, total, 0.0)

    each(tiles, rest)


def second_kernel(c1, c2, t1_own, above, below, t1, e1, t2, top, bottom, sums, va, vb):
    tiles = c1.shape[-1] // T

    def fill(j):
        sl = tile(j)
        gather_rows(t1, t1_own, above, below, j, 1)
        for r in range(1, EXT - 1):
            for p in range(2):
                va[r, p, :, sl] = c1[r, SWEEP_W, p, :, sl] * t1[r, p, :, sl]

    each(tiles, fill)
    smooth(c1, t1, va, vb, 1, EXT - 1, above.at[1], below.at[1])
    sums[...] = jnp.zeros_like(sums)

    def rest(j):
        sl = tile(j)
        total = jnp.zeros((8, T), F32)
        for r in range(WIDE, WIDE + ROWS):
            res = [t1[r, p, :, sl] - out for p, out in enumerate(apply_at(c1, r, vb, j))]
            total = total + res[0] * res[0] + res[1] * res[1]
            for p in range(2):
                e1[r - WIDE, p, :, sl] = vb[r, p, :, sl]
            val = res[0] + res[1]
            t2[r - WIDE, 0, :, sl] = val

            def product(k):
                return c2[r, k, 0, :, sl] * c2[r, SWEEP_W, 0, :, sl] * val

            send_rows(top, bottom, r - WIDE, 0, sl, val, WIDE, product)
        sums[...] += jnp.where(j < tiles - 1, total, 0.0)

    each(tiles, rest)


def third_kernel(main, c1, far, t2_own, above, below, e1_in, e1, top, bottom, t2, va, vb):
    tiles = main.shape[-1] // T
    c2 = WithFar(main, far)

    def fill(j):
        sl = tile(j)
        gather_rows(t2, t2_own, above, below, j, WIDE)
        for r in range(EXT):
            va[r, 0, :, sl] = c2[r, SWEEP_W, 0, :, sl] * t2[r, 0, :, sl]

    each(tiles, fill)
    smooth(c2, t2, va, vb, 0, EXT, above.at[WIDE], below.at[WIDE])
    smooth(c2, t2, vb, va, 1, EXT - 1)
    smooth(c2, t2, va, vb, WIDE, WIDE + ROWS)

    def last(j):
        sl = tile(j)
        for r in range(WIDE, WIDE + ROWS):
            for p in range(2):
                val = e1_in[r - WIDE, p, :, sl] + vb[r, 0, :, sl]
                e1[r - WIDE, p, :, sl] = val
                send_rows(top, bottom, r - WIDE, p, sl, val, 1, lambda k: c1[r, k, p, :, sl] * val)

    each(tiles, last)


def fourth_kernel(c1, main, t1, e1, above, below, v2, v, top, bottom, va, vb):
    tiles = c1.shape[-1] // T
    each(tiles, lambda j: gather_rows(va, e1, above, below, j, 1, c1))
    smooth(c1, t1, va, vb, 1, EXT - 1, above.at[1], below.at[1])
    smooth(c1, t1, vb, va, WIDE, WIDE + ROWS)

    def last(j):
        sl = tile(j)
        for r in range(ROWS):
            for p in range(PHASES):
                add = jnp.where(main[r, SWEEP_W, p, :, sl] != 0.0, va[r + WIDE, p // 2, :, sl], 0.0)
                val = v2[r, p, :, sl] + add
                v[r, p, :, sl] = val
                send_rows(top, bottom, r, p, sl, val, WIDE, lambda k: main[r, k, p, :, sl] * val)

    each(tiles, last)


def fifth_kernel(main, near, far, v, above, below, order, adjoint, residual, sums, va, vb, buf):
    tiles = main.shape[-1] // T
    c0 = FineRows(main, near, far)
    t0 = SourceOf(c0)
    each(tiles, lambda j: gather_rows(va, v, above, below, j, WIDE, c0))
    smooth(c0, t0, va, vb, 0, EXT, above.at[WIDE], below.at[WIDE])
    smooth(c0, t0, vb, va, 1, EXT - 1)
    sums[...] = jnp.zeros_like(sums)

    def rest(j):
        sl = tile(j)
        total = jnp.zeros((8, T), F32)
        for r in range(WIDE, WIDE + ROWS):
            for p, out in enumerate(apply_at(c0, r, va, j)):
                diff = t0[r, p, :, sl] - out
                res = jnp.where(c0[r, SWEEP_W, p, :, sl] != 0.0, diff, 0.0)
                total = total + res * res
                buf[j, p, pl.ds(r - WIDE, FIELDS, stride=ROWS), :] = va[r, p, 0:FIELDS, sl]
                buf[j, p, pl.ds(GRID + r - WIDE, FIELDS, stride=ROWS), :] = res[0:FIELDS]
        sums[...] += total

    each(tiles - 1, rest)
    x = jnp.concatenate([jnp.concatenate([buf[j, p] for p in range(PHASES)], axis=1) for j in range(tiles - 1)], axis=0)
    y = reorder(x, order[...])
    for j in range(tiles - 1):
        cols = slice(j * BLOCK, j * BLOCK + BLOCK)
        adjoint[:, cols] = y[2 * j * GRID : (2 * j + 1) * GRID]
        residual[:, cols] = y[(2 * j + 1) * GRID : (2 * j + 2) * GRID]


def call(kernel, outs, args, scratch=(), spaces=None, size=0, limit=LIMIT, out_spaces=None):
    spaces = spaces or {}
    return pl.pallas_call(
        kernel,
        out_shape=[jax.ShapeDtypeStruct(s, F32) if isinstance(s, tuple) else s for s in outs],
        in_specs=[pl.BlockSpec(memory_space=spaces.get(i, pltpu.VMEM)) for i in range(len(args))],
        out_specs=[pl.BlockSpec(memory_space=(out_spaces or {}).get(i, pltpu.VMEM)) for i in range(len(outs))],
        scratch_shapes=[pltpu.VMEM(s, F32) if isinstance(s, tuple) else s for s in scratch],
        compiler_params=pltpu.CompilerParams(vmem_limit_bytes=limit),
        cost_estimate=pl.CostEstimate(flops=0, bytes_accessed=size, transcendentals=0),
        name=kernel.__name__,
    )(*args)


def ring(x, axis, step):
    count = lax.axis_size(axis)
    return lax.ppermute(x, axis, [(i, (i + step) % count) for i in range(count)])


def total_over_devices(x):
    axes = ("hull", "blk")
    count = lax.axis_size(axes)
    sent = jnp.broadcast_to(jnp.pad(x, (0, T - x.size))[None], (count, T))
    return jnp.sum(lax.all_to_all(sent, axes, 0, 0, tiled=True), axis=0)[: x.size]


def on_device(source, jacobian, face_coef, active):
    columns = source.shape[2]
    quads = columns // PHASES
    wide = quads + T
    blocks = columns // BLOCK
    hull, blk = lax.axis_index("hull"), lax.axis_index("blk")
    ends = jnp.stack([hull > 0, hull < lax.axis_size("hull") - 1, blk > 0, blk < lax.axis_size("blk") - 1]).astype(F32)

    def cells(rows, phases):
        return (rows, phases, 8, wide)

    def coefs(rows, planes, phases):
        return (rows, planes, phases, 8, wide)

    flag = {0: pltpu.SMEM}
    inputs = [
        jacobian.reshape(FIELDS, GRID, columns),
        face_coef.reshape(4, GRID, columns),
        source.reshape(GRID, columns),
        active,
    ]
    in_hbm = {i: pltpu.HBM for i in range(len(inputs))}
    staged = [(RAW, columns), pltpu.VMEM((ROWS, columns), jnp.int32)]
    copies = pltpu.SemaphoreType.DMA((blocks, PLANES + 1))
    order = jax.ShapeDtypeStruct((BLOCK, BLOCK), BF16)
    order_side = jax.ShapeDtypeStruct((2 * T, BLOCK), BF16)
    sum_tile = (8, T)

    rows = pltpu.HBM((SENT, 8, columns), F32)
    top, bottom, left, right = call(
        send_kernel,
        [rows, rows] + [(PACK + ROWS, T)] * 2,
        [pltpu.with_memory_space_constraint(x, pltpu.HBM) for x in inputs],
        [*staged, (RAW, T), (2, SENT, 8, columns), copies, pltpu.SemaphoreType.DMA((blocks, 2))],
        in_hbm,
        limit=12 * 2**20,
        out_spaces={0: pltpu.HBM, 1: pltpu.HBM},
    )
    from_right = ring(left, "blk", -1)
    from_left = ring(right, "blk", 1)
    rows_below = ring(top, "hull", -1)
    rows_above = ring(bottom, "hull", 1)
    inner, token = call(
        own_kernel,
        [pltpu.HBM((ROWS, FINE, PHASES, 8, quads), F32), sum_tile],
        inputs,
        [
            pltpu.VMEM((BLOCK, BLOCK), BF16),
            (2, PHASES, RAW, T),
            (2, PHASES, ROWS, T),
            (2, ROWS, FINE, PHASES, 8, T),
            pltpu.SemaphoreType.DMA((blocks,)),
        ],
        size=25 * 10**6,
        limit=16 * 2**20,
        out_spaces={0: pltpu.HBM},
    )
    inner = pltpu.with_memory_space_constraint(inner, pltpu.HBM)
    corner = (2, 2, PER_GROUP * 8, T)
    top, bottom = call(corner_kernel, [corner, corner], [from_right, from_left, token], spaces={2: pl.ANY})
    corner_below = ring(top, "hull", -1)
    corner_above = ring(bottom, "hull", 1)
    main, own, side = call(
        side_kernel,
        [coefs(ROWS, FINE, 4), order, order_side],
        [ends, from_right, from_left, inner],
        [(PHASES, RAW, T), (PHASES, ROWS, T), pltpu.SemaphoreType.DMA((ROWS,))],
        {0: pltpu.SMEM, 3: pltpu.HBM},
        size=9 * 10**6,
    )
    near, v2, t1, top, bottom, sum0 = call(
        first_kernel,
        [coefs(2, FINE, 4), cells(ROWS, 4), cells(ROWS, 2), cells(2, 2), cells(2, 2), sum_tile],
        [ends, main, rows_above, rows_below, corner_above, corner_below, own, side],
        [cells(EXT, 4), cells(EXT, 4), cells(2, 4), (2, blocks, PLANES * 8, BLOCK)],
        flag,
    )
    below = ring(top, "hull", -1)
    above = ring(bottom, "hull", 1)
    (far2,) = call(
        far_coarse_kernel,
        [coefs(2, PLANES, 1)],
        [ends, rows_above, rows_below, corner_above, corner_below, own, side],
        [(2, blocks, (SENT - PLANES) * 8, BLOCK)],
        flag,
        size=7 * 10**6,
    )
    far, natural = call(
        far_kernel,
        [coefs(2, FINE, 4), order],
        [ends, rows_above, rows_below, corner_above, corner_below, own, side],
        [(2, blocks, (SENT - PLANES) * 8, BLOCK)],
        flag,
        size=8 * 10**6,
    )
    c1, c2 = call(levels_kernel, [coefs(EXT, PLANES, 2), coefs(EXT, PLANES, 1)], [ends, main, near], (), flag, size=10**7)
    t1, e1, t2, top, bottom, sum1 = call(
        second_kernel,
        [cells(EXT, 2), cells(ROWS, 2), cells(ROWS, 1), cells(3, 1), cells(3, 1), sum_tile],
        [c1, c2, t1, above, below],
        [cells(EXT, 2)] * 2,
    )
    below = ring(top, "hull", -1)
    above = ring(bottom, "hull", 1)
    e1, top, bottom = call(
        third_kernel,
        [cells(ROWS, 2), cells(2, 2), cells(2, 2)],
        [c2, c1, far2, t2, above, below, e1],
        [cells(EXT, 1)] * 3,
    )
    below = ring(top, "hull", -1)
    above = ring(bottom, "hull", 1)
    v, top, bottom = call(
        fourth_kernel, [cells(ROWS, 4), cells(3, 4), cells(3, 4)], [c1, main, t1, e1, above, below, v2], [cells(EXT, 2)] * 2
    )
    below = ring(top, "hull", -1)
    above = ring(bottom, "hull", 1)
    adjoint, residual, sum2 = call(
        fifth_kernel,
        [(GRID, columns), (GRID, columns), sum_tile],
        [main, near, far, v, above, below, natural],
        [cells(EXT, 4)] * 2 + [(blocks, PHASES, 2 * GRID, T)],
    )
    squares = jnp.stack([sum0, 2.0 * sum1, sum2])
    squares = total_over_devices(jnp.sum(squares[:, :FIELDS], axis=(1, 2)))
    count = source.size * lax.axis_size("hull") * lax.axis_size("blk")
    level_rms = jnp.sqrt(squares / float(count))
    return adjoint.reshape(source.shape), residual.reshape(source.shape), level_rms


def solution(mesh):
    return jax.shard_map(
        on_device,
        mesh=mesh,
        in_specs=(
            P(None, "hull", "blk"),
            P(None, None, "hull", "blk"),
            P(None, None, "hull", "blk"),
            P("hull", "blk"),
        ),
        out_specs=(P(None, "hull", "blk"), P(None, "hull", "blk"), P()),
        check_vma=False,
    )
```

```python
import jax
import jax.numpy as jnp
from jax import lax
from jax.experimental import pallas as pl
from jax.experimental.pallas import tpu as pltpu
from jax.sharding import PartitionSpec as P

FIELDS = 7
ROWS = 8
WIDE = 2
EXT = ROWS + 2 * WIDE
T = 128
PHASES = 4
BLOCK = PHASES * T
SIDE = 8
SIDE_COLS = SIDE * PHASES
DAMP = 0.7
PLANES = 12
SWEEP_W = 11
SOURCE = 12
FINE = 13
SENT = 22
F32 = jnp.float32
BF16 = jnp.bfloat16
LIMIT = 12 * 2**20
GRID = FIELDS * ROWS
RAW = PLANES * GRID
GROUPS = T // SIDE_COLS
PACK = RAW // GROUPS
PER_GROUP = PLANES // GROUPS


def iota(shape, dim):
    return lax.broadcasted_iota(jnp.int32, shape, dim)


def tile(j):
    return pl.ds(pl.multiple_of(j * T, T), T)


def each(count, body):
    def step(j, carry):
        body(j)
        return carry

    lax.fori_loop(0, count, step, 0)


class FineRows:
    def __init__(self, main, near, far=None):
        self.main, self.near, self.far = main, near, far
        self.shape = main.shape

    def __getitem__(self, at):
        r, *rest = at
        if r in (0, EXT - 1):
            return self.far[(r // (EXT - 1), *rest)]
        if r in (1, EXT - 2):
            return self.near[(r // (EXT - 2), *rest)]
        return self.main[(r - WIDE, *rest)]


class WithFar:
    def __init__(self, main, far):
        self.main, self.far = main, far
        self.shape = main.shape

    def __getitem__(self, at):
        r, *rest = at
        if r in (0, EXT - 1):
            return self.far[(r // (EXT - 1), *rest)]
        return self.main[(r, *rest)]


class SourceOf:
    def __init__(self, c):
        self.c = c

    def __getitem__(self, at):
        r, *rest = at
        return self.c[(r, SOURCE, *rest)]


def own_order():
    rows, cols = iota((BLOCK, BLOCK), 0), iota((BLOCK, BLOCK), 1)
    return jnp.where(rows == (cols % T) * PHASES + cols // T, 1.0, 0.0).astype(BF16)


def natural_order():
    rows, cols = iota((BLOCK, BLOCK), 0), iota((BLOCK, BLOCK), 1)
    return jnp.where(cols == (rows % T) * PHASES + rows // T, 1.0, 0.0).astype(BF16)


def side_order():
    rows, cols = iota((2 * T, BLOCK), 0), iota((2 * T, BLOCK), 1)
    lane, phase = cols % T, cols // T
    at = rows % SIDE_COLS
    after = (lane < SIDE) & (rows < T) & (at == lane * PHASES + phase)
    before = (lane >= T - SIDE) & (rows >= T) & (at == (lane - T + SIDE) * PHASES + phase)
    return jnp.where(after | before, 1.0, 0.0).astype(BF16)


def group_of(x, g):
    return jnp.where(iota(x.shape, 1) % T // SIDE_COLS == g, x, 0.0)


def reorder(x, order):
    high = x.astype(BF16)
    low = (x - high.astype(F32)).astype(BF16)
    return jnp.dot(high, order, preferred_element_type=F32) + jnp.dot(low, order, preferred_element_type=F32)


def diagonal(planes):
    sub = iota(planes[0].shape, 0)
    out = planes[FIELDS - 1]
    for f in range(FIELDS - 1):
        out = jnp.where(sub == f, planes[f], out)
    return out


def with_face_sum(planes, faces):
    total = faces[0] + faces[1] + faces[2] + faces[3]
    sub = iota(total.shape, 0)
    return [jnp.where(sub == f, x + total, x) for f, x in enumerate(planes)]


def last_sublanes(planes):
    sub = iota(planes[0].shape, 0)
    out = planes[FIELDS - 1][FIELDS:8]
    for f in range(FIELDS - 1):
        out = jnp.where(sub == f, planes[f][FIELDS:8], out)
    return out


def weight_of(planes, mask):
    return jnp.where(mask > 0.0, DAMP / diagonal(planes), 0.0)


def send_kernel(jac, face, src, act, top, bottom, left, right, raw_jac, raw_face, raw_src, flags, stage, sems, out_sems):
    columns = src.shape[-1]
    per = BLOCK // T
    blocks = columns // BLOCK
    fetches = []
    for j in range(columns // T):
        cols = pl.ds(j * T, T)
        moves = [(jac.at[:, :, cols], raw_jac.at[j]), (face.at[:, :, cols], raw_face.at[j]), (src.at[:, cols], raw_src.at[j])]
        fetches.append([pltpu.make_async_copy(a, d, sems.at[j, i]) for i, (a, d) in enumerate(moves)])
    fetches[0].append(pltpu.make_async_copy(act, flags, sems.at[0, 3]))
    last = columns // T - 1
    for j in [0, last] + list(range(1, last)):
        for copy in fetches[j]:
            copy.start()
    jobs = ((0, 0, 1, 3), (1, ROWS - 1, ROWS - 2, 2))

    def rows_of(b):
        def body(i):
            j = b * per + i
            sl = tile(j)

            def row(r):
                pick = pl.ds(r, FIELDS, stride=ROWS)
                planes = [raw_jac[j, f, pick, :] for f in range(FIELDS)]
                faces = [raw_face[j, k, pick, :] for k in range(4)]
                return with_face_sum(planes, faces), faces, raw_src[j, pick, :], flags[r : r + 1, sl].astype(F32)

            for out, near, far, face_k in jobs:
                planes, faces, source, mask = row(near)
                for k, x in enumerate(planes + faces + [source]):
                    stage[out, k, 0:FIELDS, sl] = x
                stage[out, PLANES - 1, FIELDS:8, sl] = mask
                planes, faces, source, mask = row(far)
                product = faces[face_k] * weight_of(planes, mask) * source
                for k, x in enumerate(planes + [faces[0], faces[1], faces[face_k]]):
                    stage[out, PLANES + k, 0:FIELDS, sl] = x
                for g in range(FIELDS):
                    stage[out, g, FIELDS:8, sl] = product[g : g + 1]
                    stage[out, PLANES + g, FIELDS:8, sl] = source[g : g + 1]
                stage[out, PLANES + FIELDS, FIELDS:8, sl] = mask

        each(per, body)

    def raw_plane(k, j):
        if k < FIELDS:
            return raw_jac[j, k]
        return raw_face[j, k - FIELDS] if k < PLANES - 1 else raw_src[j]

    def pack():
        lane = iota((PACK, T), 1) // SIDE_COLS
        for out, at, move in ((left, 0, 0), (right, columns - T, SIDE_COLS)):
            packed = None
            for g in range(GROUPS):
                planes = range(g * PER_GROUP, g * PER_GROUP + PER_GROUP)
                part = jnp.concatenate([raw_plane(k, at // T) for k in planes], axis=0)
                shift = (g * SIDE_COLS + move) % T
                part = pltpu.roll(part, shift, 1) if shift else part
                packed = part if packed is None else jnp.where(lane == g, part, packed)
            out[0:PACK] = packed
            mask = flags[:, at : at + T].astype(F32)
            out[PACK : PACK + ROWS] = pltpu.roll(mask, move, 1) if move else mask

    copies = []
    for copy in fetches[0] + fetches[last]:
        copy.wait()
    pack()
    for b in range(blocks):
        for j in range(b * per, b * per + per):
            if j not in (0, last):
                for copy in fetches[j]:
                    copy.wait()
        rows_of(b)
        cols = pl.ds(b * BLOCK, BLOCK)
        for i, out in enumerate((top, bottom)):
            copies.append(pltpu.make_async_copy(stage.at[i, :, :, cols], out.at[:, :, cols], out_sems.at[b, i]))
            copies[-1].start()
    for copy in copies:
        copy.wait()


def place(buf, masks, out, sl, domain):
    for r in range(ROWS):
        for p in range(PHASES):
            def pick(k):
                return buf[p, pl.ds(k * GRID + r, FIELDS, stride=ROWS), :]

            faces = [pick(FIELDS + k) for k in range(4)]
            planes = with_face_sum([pick(f) for f in range(FIELDS)], faces)
            mask = masks[p, r : r + 1, :]
            if domain is not None:
                mask = jnp.where(domain > 0.0, mask, 0.0)
            for k, x in enumerate(planes + faces + [weight_of(planes, mask), pick(PLANES - 1)]):
                out[r, k, p, 0:FIELDS, sl] = x


def side_domain(ends):
    lane = iota((1, T), 1)
    return jnp.where(lane < SIDE, ends[3], jnp.where(lane >= T - SIDE, ends[2], 0.0))


def corner_kernel(from_right, from_left, token, top, bottom):
    for side, packed in enumerate((from_right, from_left)):
        for out, rows in ((top, (0, 1)), (bottom, (ROWS - 1, ROWS - 2))):
            for i, r in enumerate(rows):
                for k in range(PER_GROUP):
                    out[i, side, k * 8 : k * 8 + FIELDS] = packed[pl.ds(k * GRID + r, FIELDS, stride=ROWS), :]
                out[i, side, FIELDS : FIELDS + 1] = packed[PACK + r : PACK + r + 1]


def corner_planes(corners, order):
    parts = [jnp.concatenate([c[i, 0], c[i, 1]], axis=1) for c in corners for i in range(2)]
    both = jnp.concatenate(parts, axis=0)
    size = PER_GROUP * 8
    every = reorder(jnp.concatenate([group_of(both, g) for g in range(GROUPS)], axis=0), order)
    packs = [every[g * both.shape[0] : (g + 1) * both.shape[0]] for g in range(GROUPS)]
    result = []
    for n in range(len(parts)):
        def plane(k, p):
            first = n * size + k % PER_GROUP * 8
            return packs[k // PER_GROUP][first : first + 8, p * T : p * T + T]

        planes = [[plane(k, p) for p in range(PHASES)] for k in range(PLANES)]
        masks = [planes[0][p][FIELDS : FIELDS + 1] for p in range(PHASES)]
        result.append((planes, masks))
    return result


def side_kernel(ends, from_right, from_left, own, main, order_own, order, buf, masks, sems):
    inner = own.shape[-1]
    half = ROWS // 2
    copies = [
        pltpu.make_async_copy(own.at[pl.ds(r, half)], main.at[pl.ds(r, half), :, :, :, pl.ds(0, inner)], sems.at[r])
        for r in (0, half)
    ]
    for copy in copies:
        copy.start()
    order[...] = side_order()
    order_own[...] = own_order()
    both = jnp.concatenate([from_right[...], from_left[...]], axis=1)
    every = reorder(jnp.concatenate([group_of(both, g) for g in range(GROUPS)], axis=0), order[...])
    for g in range(GROUPS):
        x = every[g * (PACK + ROWS) : (g + 1) * (PACK + ROWS)]
        for p in range(PHASES):
            buf[p, g * PACK : g * PACK + PACK] = x[0:PACK, p * T : p * T + T]
            if g == 0:
                masks[p] = x[PACK : PACK + ROWS, p * T : p * T + T]
    place(buf, masks, main, slice(inner, inner + T), side_domain(ends))
    for copy in copies:
        copy.wait()


def own_kernel(jac, face, src, act, own, token, order, buf, masks, stage, out_sems):
    order[...] = own_order()
    token[...] = jnp.zeros_like(token)
    outs = []
    for b in range(src.shape[-1] // BLOCK):
        cols = slice(b * BLOCK, b * BLOCK + BLOCK)
        parts = [jac[f, :, cols] for f in range(FIELDS)] + [face[k, :, cols] for k in range(4)] + [src[:, cols]]
        x = reorder(jnp.concatenate(parts, axis=0), order[...])
        m = jnp.dot(act[:, cols].astype(F32).astype(BF16), order[...], preferred_element_type=F32)
        for p in range(PHASES):
            buf[b % 2, p] = x[:, p * T : p * T + T]
            masks[b % 2, p] = m[:, p * T : p * T + T]
        if b >= 2:
            outs[b - 2].wait()
        place(buf.at[b % 2], masks.at[b % 2], stage.at[b % 2], slice(0, T), None)
        outs.append(pltpu.make_async_copy(stage.at[b % 2], own.at[:, :, :, :, pl.ds(b * T, T)], out_sems.at[b]))
        outs[b].start()
    for copy in outs[-2:]:
        copy.wait()


def row_flag(ends, r):
    if r < WIDE:
        return ends[0]
    if r >= WIDE + ROWS:
        return ends[1]
    return None


def merge(fine):
    count = len(fine[0]) // 2
    sub = iota(fine[0][0].shape, 0)
    f0, f1, f2, f3 = fine[FIELDS : FIELDS + 4]
    inner = [f1[2 * p + 1] + f0[2 * p] for p in range(count)]
    coarse = []
    for f in range(FIELDS):
        both = [fine[f][2 * p] + fine[f][2 * p + 1] for p in range(count)]
        coarse.append([jnp.where(sub == f, both[p] - inner[p], both[p]) for p in range(count)])
    coarse.append([f0[2 * p + 1] for p in range(count)])
    coarse.append([f1[2 * p] for p in range(count)])
    coarse.append([f2[2 * p] + f2[2 * p + 1] for p in range(count)])
    coarse.append([f3[2 * p] + f3[2 * p + 1] for p in range(count)])
    return coarse


def build_levels(read, outs, sl, domain):
    fine = [[read(k, p) for p in range(PHASES)] for k in range(PLANES - 1)]
    for write in outs:
        fine = merge(fine)
        for p in range(len(fine[0])):
            weight = DAMP / diagonal([fine[f][p] for f in range(FIELDS)])
            if domain is not None:
                weight = jnp.where(domain > 0.0, weight, 0.0)
            if write is not None:
                for k, planes in enumerate(fine):
                    write(k, p, planes[p])
                write(SWEEP_W, p, weight)


def levels_kernel(ends, main, near, c1, c2):
    tiles = main.shape[-1] // T
    sides = side_domain(ends)

    def build(source, row, r, sl, domain):
        def put(out):
            def write(k, p, x):
                out[r, k, p, :, sl] = x

            return write

        build_levels(lambda k, p: source[row, k, p, :, sl], [put(c1), put(c2)], sl, domain)

    def body(r):
        each(tiles - 1, lambda j: build(main, r, r + WIDE, tile(j), None))

    each(ROWS, body)
    sl = slice((tiles - 1) * T, tiles * T)
    each(ROWS, lambda r: build(main, r, r + WIDE, sl, sides))
    for i, r in enumerate((1, EXT - 2)):
        each(tiles - 1, lambda j: build(near, i, r, tile(j), row_flag(ends, r)))
        build(near, i, r, sl, sides * row_flag(ends, r))


def far_planes(ends, rows, corners, wide, put):
    def fill(j):
        for i in range(2):
            cells = []
            for p in range(PHASES):
                planes = [rows[i, j, k * 8 : k * 8 + 8, p * T : p * T + T] for k in range(SENT - PLANES)]
                mask = planes[FIELDS][FIELDS:8] * ends[i]
                cells.append((planes[:FIELDS], planes[FIELDS:], planes, mask))
            put(i, cells, tile(j), ends[i])

    each(wide // T - 1, fill)
    for i in range(2):
        domain = side_domain(ends) * ends[i]
        planes, masks = corners[2 * i + 1]
        cells = []
        for p in range(PHASES):
            raw = [x[p] for x in planes]
            faces = raw[FIELDS : FIELDS + 4]
            mask = jnp.where(domain > 0.0, masks[p], 0.0)
            cells.append((with_face_sum(raw[:FIELDS], faces), [faces[0], faces[1], faces[2 + i]], raw[PLANES - 1], mask))
        put(i, cells, slice(wide - T, wide), domain)


def far_kernel(ends, rows_above, rows_below, corner_above, corner_below, order, order_side, far, order_out, rows):
    order_out[...] = natural_order()
    reorder_rows(rows_above, rows_below, slice(PLANES, SENT), order[...], rows)

    def put(i, cells, sl, domain):
        for p, (planes, faces, source, mask) in enumerate(cells):
            for k, x in enumerate(planes + faces[:2]):
                far[i, k, p, :, sl] = x
            far[i, FIELDS + 2 + i, p, :, sl] = faces[2]
            far[i, SWEEP_W, p, :, sl] = weight_of(planes, mask)
            far[i, SOURCE, p, :, sl] = last_sublanes(source) if isinstance(source, list) else source

    corners = corner_planes((corner_above, corner_below), order_side[...])
    far_planes(ends, rows, corners, far.shape[-1], put)


def far_coarse_kernel(ends, rows_above, rows_below, corner_above, corner_below, order, order_side, far, rows):
    reorder_rows(rows_above, rows_below, slice(PLANES, SENT), order[...], rows)

    def put(i, cells, sl, domain):
        def read(k, p):
            planes, faces, _, _ = cells[p]
            return planes[k] if k < FIELDS else faces[min(k - FIELDS, 2)]

        def write(k, p, x):
            if k in (FIELDS + 2, FIELDS + 3) and k != FIELDS + 2 + i:
                return
            far[i, k, p, :, sl] = x

        build_levels(read, [None, write], sl, domain)

    corners = corner_planes((corner_above, corner_below), order_side[...])
    far_planes(ends, rows, corners, far.shape[-1], put)


def apply_at(c, r, v, j, above=None, below=None):
    tiles = c.shape[-1] // T
    count = c.shape[2]
    sl = tile(j)
    before = tile(lax.rem(j + tiles - 1, tiles))
    after = tile(lax.rem(j + 1, tiles))
    lane = iota((8, T), 1)
    here = [v[r, p, :, sl] for p in range(count)]
    k = FIELDS
    east = [c[r, k, p, :, sl] * here[p] for p in range(count)]
    west = [c[r, k + 1, p, :, sl] * here[p] for p in range(count)]
    end = count - 1
    wrap = jnp.where(lane == T - 1, c[r, k, end, :, before] * v[r, end, :, before], east[end])
    from_left = [pltpu.roll(wrap, 1, 1)] + east[:end]
    wrap = jnp.where(lane == 0, c[r, k + 1, 0, :, after] * v[r, 0, :, after], west[0])
    from_right = west[1:] + [pltpu.roll(wrap, T - 1, 1)]
    outs = []
    for p in range(count):
        out = c[r, 0, p, :, sl] * v[r, p, 0:1, sl]
        for f in range(1, FIELDS):
            out = out + c[r, f, p, :, sl] * v[r, p, f : f + 1, sl]
        up = c[r - 1, k + 2, p, :, sl] * v[r - 1, p, :, sl] if above is None else above[p, :, sl]
        down = c[r + 1, k + 3, p, :, sl] * v[r + 1, p, :, sl] if below is None else below[p, :, sl]
        outs.append(out - (from_left[p] + from_right[p]) - (up + down))
    return outs


def smooth(c, t, old, new, first, last, above=None, below=None):
    def body(j):
        sl = tile(j)
        for r in range(first, last):
            up = above if r == first else None
            down = below if r == last - 1 else None
            for p, out in enumerate(apply_at(c, r, old, j, up, down)):
                diff = t[r, p, :, sl] - out
                new[r, p, :, sl] = old[r, p, :, sl] + diff * c[r, SWEEP_W, p, :, sl]

    each(c.shape[-1] // T, body)


def gather_rows(out, own, above, below, j, wide, weight=None):
    sl = tile(j)
    for r in range(WIDE - wide, WIDE + ROWS + wide):
        for p in range(out.shape[1]):
            if r < WIDE:
                val = above[WIDE - 1 - r, p, :, sl]
            elif r < WIDE + ROWS:
                val = own[r - WIDE, p, :, sl]
            else:
                val = below[r - WIDE - ROWS, p, :, sl]
            if weight is not None and not WIDE <= r < WIDE + ROWS:
                val = jnp.where(weight[r, SWEEP_W, p, :, sl] != 0.0, val, 0.0)
            out[r, p, :, sl] = val


def send_rows(top, bottom, row, p, sl, val, wide, product):
    if row < wide:
        top[row, p, :, sl] = val
    if row >= ROWS - wide:
        bottom[ROWS - 1 - row, p, :, sl] = val
    if row == wide:
        top[wide, p, :, sl] = product(FIELDS + 3)
    if row == ROWS - 1 - wide:
        bottom[wide, p, :, sl] = product(FIELDS + 2)


def reorder_rows(rows_above, rows_below, planes, order, out):
    blocks = rows_above.shape[-1] // BLOCK
    size = (planes.stop - planes.start) * 8
    parts = [rows[planes, :, b * BLOCK : b * BLOCK + BLOCK].reshape(size, BLOCK) for rows in (rows_above, rows_below) for b in range(blocks)]
    x = reorder(jnp.concatenate(parts, axis=0), order)
    for n in range(len(parts)):
        out[n // blocks, n % blocks] = x[n * size : n * size + size]


def first_kernel(ends, main, rows_above, rows_below, corner_above, corner_below, order, order_side, near, v2, t1, t1_top, t1_bottom, sums, va, vb, prods, rows):
    tiles = main.shape[-1] // T
    c0 = FineRows(main, near)
    t0 = SourceOf(c0)
    last = slice((tiles - 1) * T, tiles * T)

    def put(i, p, planes, mask, sl):
        source = planes[PLANES - 1]
        weight = weight_of(planes[:FIELDS], mask)
        for k, x in enumerate(planes[: PLANES - 1] + [weight, source]):
            near[i, k, p, :, sl] = x
        va[1 if i == 0 else EXT - 2, p, :, sl] = weight * source

    def fill(j):
        sl = tile(j)
        for i in range(2):
            for p in range(PHASES):
                planes = [rows[i, j, k * 8 : k * 8 + 8, p * T : p * T + T] for k in range(PLANES)]
                put(i, p, planes, planes[PLANES - 1][FIELDS:8] * ends[i], sl)
                prods[i, p, :, sl] = last_sublanes(planes)

    reorder_rows(rows_above, rows_below, slice(0, PLANES), order[...], rows)
    each(tiles - 1, fill)
    sides = side_domain(ends)
    corners = corner_planes((corner_above, corner_below), order_side[...])
    for i in range(2):
        domain = sides * ends[i]
        planes, masks = corners[2 * i]
        far, far_masks = corners[2 * i + 1]
        for p in range(PHASES):
            raw = [x[p] for x in planes]
            raw[:FIELDS] = with_face_sum(raw[:FIELDS], raw[FIELDS : FIELDS + 4])
            put(i, p, raw, jnp.where(domain > 0.0, masks[p], 0.0), last)
            here = [x[p] for x in far]
            jac = with_face_sum(here[:FIELDS], here[FIELDS : FIELDS + 4])
            weight = weight_of(jac, jnp.where(domain > 0.0, far_masks[p], 0.0))
            prods[i, p, :, last] = here[FIELDS + 2 + i] * weight * here[PLANES - 1]

    def own(j):
        sl = tile(j)
        for r in range(WIDE, WIDE + ROWS):
            for p in range(PHASES):
                va[r, p, :, sl] = c0[r, SWEEP_W, p, :, sl] * t0[r, p, :, sl]

    each(tiles, own)

    smooth(c0, t0, va, vb, 1, EXT - 1, prods.at[0], prods.at[1])
    sums[...] = jnp.zeros_like(sums)

    def rest(j):
        sl = tile(j)
        total = jnp.zeros((8, T), F32)
        for r in range(WIDE, WIDE + ROWS):
            res = []
            for p, out in enumerate(apply_at(c0, r, vb, j)):
                diff = t0[r, p, :, sl] - out
                res.append(jnp.where(c0[r, SWEEP_W, p, :, sl] != 0.0, diff, 0.0))
                total = total + res[p] * res[p]
                v2[r - WIDE, p, :, sl] = vb[r, p, :, sl]
            row = r - WIDE
            if row in (1, ROWS - 2):
                coarse = merge([[c0[r, k, p, :, sl] for p in range(PHASES)] for k in range(PLANES - 1)])
            for p in range(PHASES // 2):
                val = res[2 * p] + res[2 * p + 1]
                t1[row, p, :, sl] = val

                def product(k):
                    diag = diagonal([coarse[f][p] for f in range(FIELDS)])
                    return coarse[k][p] * jnp.where(diag > 0.0, DAMP / diag, 0.0) * val

                send_rows(t1_top, t1_bottom, row, p, sl, val, 1, product)
        sums[...] += jnp.where(j < tiles - 1, total, 0.0)

    each(tiles, rest)


def second_kernel(c1, c2, t1_own, above, below, t1, e1, t2, top, bottom, sums, va, vb):
    tiles = c1.shape[-1] // T

    def fill(j):
        sl = tile(j)
        gather_rows(t1, t1_own, above, below, j, 1)
        for r in range(1, EXT - 1):
            for p in range(2):
                va[r, p, :, sl] = c1[r, SWEEP_W, p, :, sl] * t1[r, p, :, sl]

    each(tiles, fill)
    smooth(c1, t1, va, vb, 1, EXT - 1, above.at[1], below.at[1])
    sums[...] = jnp.zeros_like(sums)

    def rest(j):
        sl = tile(j)
        total = jnp.zeros((8, T), F32)
        for r in range(WIDE, WIDE + ROWS):
            res = [t1[r, p, :, sl] - out for p, out in enumerate(apply_at(c1, r, vb, j))]
            total = total + res[0] * res[0] + res[1] * res[1]
            for p in range(2):
                e1[r - WIDE, p, :, sl] = vb[r, p, :, sl]
            val = res[0] + res[1]
            t2[r - WIDE, 0, :, sl] = val

            def product(k):
                return c2[r, k, 0, :, sl] * c2[r, SWEEP_W, 0, :, sl] * val

            send_rows(top, bottom, r - WIDE, 0, sl, val, WIDE, product)
        sums[...] += jnp.where(j < tiles - 1, total, 0.0)

    each(tiles, rest)


def third_kernel(main, c1, far, t2_own, above, below, e1_in, e1, top, bottom, t2, va, vb):
    tiles = main.shape[-1] // T
    c2 = WithFar(main, far)

    def fill(j):
        sl = tile(j)
        gather_rows(t2, t2_own, above, below, j, WIDE)
        for r in range(EXT):
            va[r, 0, :, sl] = c2[r, SWEEP_W, 0, :, sl] * t2[r, 0, :, sl]

    each(tiles, fill)
    smooth(c2, t2, va, vb, 0, EXT, above.at[WIDE], below.at[WIDE])
    smooth(c2, t2, vb, va, 1, EXT - 1)
    smooth(c2, t2, va, vb, WIDE, WIDE + ROWS)

    def last(j):
        sl = tile(j)
        for r in range(WIDE, WIDE + ROWS):
            for p in range(2):
                val = e1_in[r - WIDE, p, :, sl] + vb[r, 0, :, sl]
                e1[r - WIDE, p, :, sl] = val
                send_rows(top, bottom, r - WIDE, p, sl, val, 1, lambda k: c1[r, k, p, :, sl] * val)

    each(tiles, last)


def fourth_kernel(c1, main, t1, e1, above, below, v2, v, top, bottom, va, vb):
    tiles = c1.shape[-1] // T
    each(tiles, lambda j: gather_rows(va, e1, above, below, j, 1, c1))
    smooth(c1, t1, va, vb, 1, EXT - 1, above.at[1], below.at[1])
    smooth(c1, t1, vb, va, WIDE, WIDE + ROWS)

    def last(j):
        sl = tile(j)
        for r in range(ROWS):
            for p in range(PHASES):
                add = jnp.where(main[r, SWEEP_W, p, :, sl] != 0.0, va[r + WIDE, p // 2, :, sl], 0.0)
                val = v2[r, p, :, sl] + add
                v[r, p, :, sl] = val
                send_rows(top, bottom, r, p, sl, val, WIDE, lambda k: main[r, k, p, :, sl] * val)

    each(tiles, last)


def fifth_kernel(main, near, far, v, above, below, order, adjoint, residual, sums, va, vb, buf):
    tiles = main.shape[-1] // T
    c0 = FineRows(main, near, far)
    t0 = SourceOf(c0)
    each(tiles, lambda j: gather_rows(va, v, above, below, j, WIDE, c0))
    smooth(c0, t0, va, vb, 0, EXT, above.at[WIDE], below.at[WIDE])
    smooth(c0, t0, vb, va, 1, EXT - 1)
    sums[...] = jnp.zeros_like(sums)

    def rest(j):
        sl = tile(j)
        total = jnp.zeros((8, T), F32)
        for r in range(WIDE, WIDE + ROWS):
            for p, out in enumerate(apply_at(c0, r, va, j)):
                diff = t0[r, p, :, sl] - out
                res = jnp.where(c0[r, SWEEP_W, p, :, sl] != 0.0, diff, 0.0)
                total = total + res * res
                buf[j, p, pl.ds(r - WIDE, FIELDS, stride=ROWS), :] = va[r, p, 0:FIELDS, sl]
                buf[j, p, pl.ds(GRID + r - WIDE, FIELDS, stride=ROWS), :] = res[0:FIELDS]
        sums[...] += total

    each(tiles - 1, rest)
    x = jnp.concatenate([jnp.concatenate([buf[j, p] for p in range(PHASES)], axis=1) for j in range(tiles - 1)], axis=0)
    y = reorder(x, order[...])
    for j in range(tiles - 1):
        cols = slice(j * BLOCK, j * BLOCK + BLOCK)
        adjoint[:, cols] = y[2 * j * GRID : (2 * j + 1) * GRID]
        residual[:, cols] = y[(2 * j + 1) * GRID : (2 * j + 2) * GRID]


def call(kernel, outs, args, scratch=(), spaces=None, size=0, limit=LIMIT, out_spaces=None):
    spaces = spaces or {}
    return pl.pallas_call(
        kernel,
        out_shape=[jax.ShapeDtypeStruct(s, F32) if isinstance(s, tuple) else s for s in outs],
        in_specs=[pl.BlockSpec(memory_space=spaces.get(i, pltpu.VMEM)) for i in range(len(args))],
        out_specs=[pl.BlockSpec(memory_space=(out_spaces or {}).get(i, pltpu.VMEM)) for i in range(len(outs))],
        scratch_shapes=[pltpu.VMEM(s, F32) if isinstance(s, tuple) else s for s in scratch],
        compiler_params=pltpu.CompilerParams(vmem_limit_bytes=limit),
        cost_estimate=pl.CostEstimate(flops=0, bytes_accessed=size, transcendentals=0),
        name=kernel.__name__,
    )(*args)


def ring(x, axis, step):
    count = lax.axis_size(axis)
    return lax.ppermute(x, axis, [(i, (i + step) % count) for i in range(count)])


def total_over_devices(x):
    axes = ("hull", "blk")
    count = lax.axis_size(axes)
    sent = jnp.broadcast_to(jnp.pad(x, (0, T - x.size))[None], (count, T))
    return jnp.sum(lax.all_to_all(sent, axes, 0, 0, tiled=True), axis=0)[: x.size]


def on_device(source, jacobian, face_coef, active):
    columns = source.shape[2]
    quads = columns // PHASES
    wide = quads + T
    blocks = columns // BLOCK
    hull, blk = lax.axis_index("hull"), lax.axis_index("blk")
    ends = jnp.stack([hull > 0, hull < lax.axis_size("hull") - 1, blk > 0, blk < lax.axis_size("blk") - 1]).astype(F32)

    def cells(rows, phases):
        return (rows, phases, 8, wide)

    def coefs(rows, planes, phases):
        return (rows, planes, phases, 8, wide)

    flag = {0: pltpu.SMEM}
    inputs = [
        jacobian.reshape(FIELDS, GRID, columns),
        face_coef.reshape(4, GRID, columns),
        source.reshape(GRID, columns),
        active,
    ]
    in_hbm = {i: pltpu.HBM for i in range(len(inputs))}
    tiles = columns // T
    staged = [(tiles, FIELDS, GRID, T), (tiles, 4, GRID, T), (tiles, GRID, T), pltpu.VMEM((ROWS, columns), jnp.int32)]
    order = jax.ShapeDtypeStruct((BLOCK, BLOCK), BF16)
    order_side = jax.ShapeDtypeStruct((2 * T, BLOCK), BF16)
    sum_tile = (8, T)

    rows = pltpu.HBM((SENT, 8, columns), F32)
    top, bottom, left, right = call(
        send_kernel,
        [rows, rows] + [(PACK + ROWS, T)] * 2,
        [pltpu.with_memory_space_constraint(x, pltpu.HBM) for x in inputs],
        [*staged, (2, SENT, 8, columns), pltpu.SemaphoreType.DMA((tiles, 4)), pltpu.SemaphoreType.DMA((blocks, 2))],
        in_hbm,
        limit=12 * 2**20,
        out_spaces={0: pltpu.HBM, 1: pltpu.HBM},
    )
    from_right = ring(left, "blk", -1)
    from_left = ring(right, "blk", 1)
    rows_below = ring(top, "hull", -1)
    rows_above = ring(bottom, "hull", 1)
    inner, token = call(
        own_kernel,
        [pltpu.HBM((ROWS, FINE, PHASES, 8, quads), F32), sum_tile],
        inputs,
        [
            pltpu.VMEM((BLOCK, BLOCK), BF16),
            (2, PHASES, RAW, T),
            (2, PHASES, ROWS, T),
            (2, ROWS, FINE, PHASES, 8, T),
            pltpu.SemaphoreType.DMA((blocks,)),
        ],
        size=25 * 10**6,
        limit=16 * 2**20,
        out_spaces={0: pltpu.HBM},
    )
    inner = pltpu.with_memory_space_constraint(inner, pltpu.HBM)
    corner = (2, 2, PER_GROUP * 8, T)
    top, bottom = call(corner_kernel, [corner, corner], [from_right, from_left, token], spaces={2: pl.ANY})
    corner_below = ring(top, "hull", -1)
    corner_above = ring(bottom, "hull", 1)
    main, own, side = call(
        side_kernel,
        [coefs(ROWS, FINE, 4), order, order_side],
        [ends, from_right, from_left, inner],
        [(PHASES, RAW, T), (PHASES, ROWS, T), pltpu.SemaphoreType.DMA((ROWS,))],
        {0: pltpu.SMEM, 3: pltpu.HBM},
        size=9 * 10**6,
    )
    near, v2, t1, top, bottom, sum0 = call(
        first_kernel,
        [coefs(2, FINE, 4), cells(ROWS, 4), cells(ROWS, 2), cells(2, 2), cells(2, 2), sum_tile],
        [ends, main, rows_above, rows_below, corner_above, corner_below, own, side],
        [cells(EXT, 4), cells(EXT, 4), cells(2, 4), (2, blocks, PLANES * 8, BLOCK)],
        flag,
    )
    below = ring(top, "hull", -1)
    above = ring(bottom, "hull", 1)
    (far2,) = call(
        far_coarse_kernel,
        [coefs(2, PLANES, 1)],
        [ends, rows_above, rows_below, corner_above, corner_below, own, side],
        [(2, blocks, (SENT - PLANES) * 8, BLOCK)],
        flag,
        size=7 * 10**6,
    )
    far, natural = call(
        far_kernel,
        [coefs(2, FINE, 4), order],
        [ends, rows_above, rows_below, corner_above, corner_below, own, side],
        [(2, blocks, (SENT - PLANES) * 8, BLOCK)],
        flag,
        size=8 * 10**6,
    )
    c1, c2 = call(levels_kernel, [coefs(EXT, PLANES, 2), coefs(EXT, PLANES, 1)], [ends, main, near], (), flag, size=10**7)
    t1, e1, t2, top, bottom, sum1 = call(
        second_kernel,
        [cells(EXT, 2), cells(ROWS, 2), cells(ROWS, 1), cells(3, 1), cells(3, 1), sum_tile],
        [c1, c2, t1, above, below],
        [cells(EXT, 2)] * 2,
    )
    below = ring(top, "hull", -1)
    above = ring(bottom, "hull", 1)
    e1, top, bottom = call(
        third_kernel,
        [cells(ROWS, 2), cells(2, 2), cells(2, 2)],
        [c2, c1, far2, t2, above, below, e1],
        [cells(EXT, 1)] * 3,
    )
    below = ring(top, "hull", -1)
    above = ring(bottom, "hull", 1)
    v, top, bottom = call(
        fourth_kernel, [cells(ROWS, 4), cells(3, 4), cells(3, 4)], [c1, main, t1, e1, above, below, v2], [cells(EXT, 2)] * 2
    )
    below = ring(top, "hull", -1)
    above = ring(bottom, "hull", 1)
    adjoint, residual, sum2 = call(
        fifth_kernel,
        [(GRID, columns), (GRID, columns), sum_tile],
        [main, near, far, v, above, below, natural],
        [cells(EXT, 4)] * 2 + [(blocks, PHASES, 2 * GRID, T)],
    )
    squares = jnp.stack([sum0, 2.0 * sum1, sum2])
    squares = total_over_devices(jnp.sum(squares[:, :FIELDS], axis=(1, 2)))
    count = source.size * lax.axis_size("hull") * lax.axis_size("blk")
    level_rms = jnp.sqrt(squares / float(count))
    return adjoint.reshape(source.shape), residual.reshape(source.shape), level_rms


def solution(mesh):
    return jax.shard_map(
        on_device,
        mesh=mesh,
        in_specs=(
            P(None, "hull", "blk"),
            P(None, None, "hull", "blk"),
            P(None, None, "hull", "blk"),
            P("hull", "blk"),
        ),
        out_specs=(P(None, "hull", "blk"), P(None, "hull", "blk"), P()),
        check_vma=False,
    )
```

```python
import jax
import jax.numpy as jnp
from jax import lax
from jax.experimental import pallas as pl
from jax.experimental.pallas import tpu as pltpu
from jax.sharding import PartitionSpec as P

FIELDS = 7
ROWS = 8
WIDE = 2
EXT = ROWS + 2 * WIDE
T = 128
PHASES = 4
BLOCK = PHASES * T
SIDE = 8
SIDE_COLS = SIDE * PHASES
DAMP = 0.7
PLANES = 12
SWEEP_W = 11
SOURCE = 12
FINE = 13
SENT = 22
F32 = jnp.float32
BF16 = jnp.bfloat16
LIMIT = 12 * 2**20
GRID = FIELDS * ROWS
RAW = PLANES * GRID
GROUPS = T // SIDE_COLS
PACK = RAW // GROUPS
PER_GROUP = PLANES // GROUPS


def iota(shape, dim):
    return lax.broadcasted_iota(jnp.int32, shape, dim)


def tile(j):
    return pl.ds(pl.multiple_of(j * T, T), T)


def each(count, body):
    def step(j, carry):
        body(j)
        return carry

    lax.fori_loop(0, count, step, 0)


class FineRows:
    def __init__(self, main, near, far=None):
        self.main, self.near, self.far = main, near, far
        self.shape = main.shape

    def __getitem__(self, at):
        r, *rest = at
        if r in (0, EXT - 1):
            return self.far[(r // (EXT - 1), *rest)]
        if r in (1, EXT - 2):
            return self.near[(r // (EXT - 2), *rest)]
        return self.main[(r - WIDE, *rest)]


class WithFar:
    def __init__(self, main, far):
        self.main, self.far = main, far
        self.shape = main.shape

    def __getitem__(self, at):
        r, *rest = at
        if r in (0, EXT - 1):
            return self.far[(r // (EXT - 1), *rest)]
        return self.main[(r, *rest)]


class SourceOf:
    def __init__(self, c):
        self.c = c

    def __getitem__(self, at):
        r, *rest = at
        return self.c[(r, SOURCE, *rest)]


def own_order():
    rows, cols = iota((BLOCK, BLOCK), 0), iota((BLOCK, BLOCK), 1)
    return jnp.where(rows == (cols % T) * PHASES + cols // T, 1.0, 0.0).astype(BF16)


def natural_order():
    rows, cols = iota((BLOCK, BLOCK), 0), iota((BLOCK, BLOCK), 1)
    return jnp.where(cols == (rows % T) * PHASES + rows // T, 1.0, 0.0).astype(BF16)


def side_order():
    rows, cols = iota((2 * T, BLOCK), 0), iota((2 * T, BLOCK), 1)
    lane, phase = cols % T, cols // T
    at = rows % SIDE_COLS
    after = (lane < SIDE) & (rows < T) & (at == lane * PHASES + phase)
    before = (lane >= T - SIDE) & (rows >= T) & (at == (lane - T + SIDE) * PHASES + phase)
    return jnp.where(after | before, 1.0, 0.0).astype(BF16)


def group_of(x, g):
    return jnp.where(iota(x.shape, 1) % T // SIDE_COLS == g, x, 0.0)


def reorder(x, order):
    high = x.astype(BF16)
    low = (x - high.astype(F32)).astype(BF16)
    return jnp.dot(high, order, preferred_element_type=F32) + jnp.dot(low, order, preferred_element_type=F32)


def diagonal(planes):
    sub = iota(planes[0].shape, 0)
    out = planes[FIELDS - 1]
    for f in range(FIELDS - 1):
        out = jnp.where(sub == f, planes[f], out)
    return out


def with_face_sum(planes, faces):
    total = faces[0] + faces[1] + faces[2] + faces[3]
    sub = iota(total.shape, 0)
    return [jnp.where(sub == f, x + total, x) for f, x in enumerate(planes)]


def last_sublanes(planes):
    sub = iota(planes[0].shape, 0)
    out = planes[FIELDS - 1][FIELDS:8]
    for f in range(FIELDS - 1):
        out = jnp.where(sub == f, planes[f][FIELDS:8], out)
    return out


def weight_of(planes, mask):
    return jnp.where(mask > 0.0, DAMP / diagonal(planes), 0.0)


def send_kernel(jac, face, src, act, top, bottom, left, right, raw_jac, raw_face, raw_src, flags, stage, sems, out_sems):
    columns = src.shape[-1]
    per = BLOCK // T
    blocks = columns // BLOCK
    fetches = []
    for j in range(columns // T):
        cols = pl.ds(j * T, T)
        moves = [(jac.at[:, :, cols], raw_jac.at[j]), (face.at[:, :, cols], raw_face.at[j]), (src.at[:, cols], raw_src.at[j])]
        fetches.append([pltpu.make_async_copy(a, d, sems.at[j, i]) for i, (a, d) in enumerate(moves)])
    fetches[0].append(pltpu.make_async_copy(act, flags, sems.at[0, 3]))
    last = columns // T - 1
    for j in [0, last] + list(range(1, last)):
        for copy in fetches[j]:
            copy.start()
    jobs = ((0, 0, 1, 3), (1, ROWS - 1, ROWS - 2, 2))

    def rows_of(b):
        def body(i):
            j = b * per + i
            sl = tile(j)

            def row(r):
                pick = pl.ds(r, FIELDS, stride=ROWS)
                planes = [raw_jac[j, f, pick, :] for f in range(FIELDS)]
                faces = [raw_face[j, k, pick, :] for k in range(4)]
                return with_face_sum(planes, faces), faces, raw_src[j, pick, :], flags[r : r + 1, sl].astype(F32)

            for out, near, far, face_k in jobs:
                planes, faces, source, mask = row(near)
                for k, x in enumerate(planes + faces + [source]):
                    stage[out, k, 0:FIELDS, sl] = x
                stage[out, PLANES - 1, FIELDS:8, sl] = mask
                planes, faces, source, mask = row(far)
                product = faces[face_k] * weight_of(planes, mask) * source
                for k, x in enumerate(planes + [faces[0], faces[1], faces[face_k]]):
                    stage[out, PLANES + k, 0:FIELDS, sl] = x
                for g in range(FIELDS):
                    stage[out, g, FIELDS:8, sl] = product[g : g + 1]
                    stage[out, PLANES + g, FIELDS:8, sl] = source[g : g + 1]
                stage[out, PLANES + FIELDS, FIELDS:8, sl] = mask

        each(per, body)

    def raw_plane(k, j):
        if k < FIELDS:
            return raw_jac[j, k]
        return raw_face[j, k - FIELDS] if k < PLANES - 1 else raw_src[j]

    def pack():
        lane = iota((PACK, T), 1) // SIDE_COLS
        for out, at, move in ((left, 0, 0), (right, columns - T, SIDE_COLS)):
            packed = None
            for g in range(GROUPS):
                planes = range(g * PER_GROUP, g * PER_GROUP + PER_GROUP)
                part = jnp.concatenate([raw_plane(k, at // T) for k in planes], axis=0)
                shift = (g * SIDE_COLS + move) % T
                part = pltpu.roll(part, shift, 1) if shift else part
                packed = part if packed is None else jnp.where(lane == g, part, packed)
            out[0:PACK] = packed
            mask = flags[:, at : at + T].astype(F32)
            out[PACK : PACK + ROWS] = pltpu.roll(mask, move, 1) if move else mask

    copies = []
    for copy in fetches[0] + fetches[last]:
        copy.wait()
    pack()
    for b in range(blocks):
        for j in range(b * per, b * per + per):
            if j not in (0, last):
                for copy in fetches[j]:
                    copy.wait()
        rows_of(b)
        cols = pl.ds(b * BLOCK, BLOCK)
        for i, out in enumerate((top, bottom)):
            copies.append(pltpu.make_async_copy(stage.at[i, :, :, cols], out.at[:, :, cols], out_sems.at[b, i]))
            copies[-1].start()
    for copy in copies:
        copy.wait()


def place(buf, masks, out, sl, domain):
    for r in range(ROWS):
        for p in range(PHASES):
            def pick(k):
                return buf[p, pl.ds(k * GRID + r, FIELDS, stride=ROWS), :]

            faces = [pick(FIELDS + k) for k in range(4)]
            planes = with_face_sum([pick(f) for f in range(FIELDS)], faces)
            mask = masks[p, r : r + 1, :]
            if domain is not None:
                mask = jnp.where(domain > 0.0, mask, 0.0)
            for k, x in enumerate(planes + faces + [weight_of(planes, mask), pick(PLANES - 1)]):
                out[r, k, p, 0:FIELDS, sl] = x


def side_domain(ends):
    lane = iota((1, T), 1)
    return jnp.where(lane < SIDE, ends[3], jnp.where(lane >= T - SIDE, ends[2], 0.0))


def corner_kernel(from_right, from_left, token, top, bottom):
    for side, packed in enumerate((from_right, from_left)):
        for out, rows in ((top, (0, 1)), (bottom, (ROWS - 1, ROWS - 2))):
            for i, r in enumerate(rows):
                for k in range(PER_GROUP):
                    out[i, side, k * 8 : k * 8 + FIELDS] = packed[pl.ds(k * GRID + r, FIELDS, stride=ROWS), :]
                out[i, side, FIELDS : FIELDS + 1] = packed[PACK + r : PACK + r + 1]


def corner_planes(corners, order):
    parts = [jnp.concatenate([c[i, 0], c[i, 1]], axis=1) for c in corners for i in range(2)]
    both = jnp.concatenate(parts, axis=0)
    size = PER_GROUP * 8
    every = reorder(jnp.concatenate([group_of(both, g) for g in range(GROUPS)], axis=0), order)
    packs = [every[g * both.shape[0] : (g + 1) * both.shape[0]] for g in range(GROUPS)]
    result = []
    for n in range(len(parts)):
        def plane(k, p):
            first = n * size + k % PER_GROUP * 8
            return packs[k // PER_GROUP][first : first + 8, p * T : p * T + T]

        planes = [[plane(k, p) for p in range(PHASES)] for k in range(PLANES)]
        masks = [planes[0][p][FIELDS : FIELDS + 1] for p in range(PHASES)]
        result.append((planes, masks))
    return result


def side_kernel(ends, from_right, from_left, own, main, order_own, order, buf, masks, sems):
    inner = own.shape[-1]
    half = ROWS // 2
    copies = [
        pltpu.make_async_copy(own.at[pl.ds(r, half)], main.at[pl.ds(r, half), :, :, :, pl.ds(0, inner)], sems.at[r])
        for r in (0, half)
    ]
    for copy in copies:
        copy.start()
    order[...] = side_order()
    order_own[...] = own_order()
    both = jnp.concatenate([from_right[...], from_left[...]], axis=1)
    every = reorder(jnp.concatenate([group_of(both, g) for g in range(GROUPS)], axis=0), order[...])
    for g in range(GROUPS):
        x = every[g * (PACK + ROWS) : (g + 1) * (PACK + ROWS)]
        for p in range(PHASES):
            buf[p, g * PACK : g * PACK + PACK] = x[0:PACK, p * T : p * T + T]
            if g == 0:
                masks[p] = x[PACK : PACK + ROWS, p * T : p * T + T]
    place(buf, masks, main, slice(inner, inner + T), side_domain(ends))
    for copy in copies:
        copy.wait()


def own_kernel(jac, face, src, act, own, token, order, buf, masks, stage, out_sems):
    order[...] = own_order()
    token[...] = jnp.zeros_like(token)
    outs = []
    for b in range(src.shape[-1] // BLOCK):
        cols = slice(b * BLOCK, b * BLOCK + BLOCK)
        parts = [jac[f, :, cols] for f in range(FIELDS)] + [face[k, :, cols] for k in range(4)] + [src[:, cols]]
        x = reorder(jnp.concatenate(parts, axis=0), order[...])
        m = jnp.dot(act[:, cols].astype(F32).astype(BF16), order[...], preferred_element_type=F32)
        for p in range(PHASES):
            buf[b % 2, p] = x[:, p * T : p * T + T]
            masks[b % 2, p] = m[:, p * T : p * T + T]
        if b >= 2:
            outs[b - 2].wait()
        place(buf.at[b % 2], masks.at[b % 2], stage.at[b % 2], slice(0, T), None)
        outs.append(pltpu.make_async_copy(stage.at[b % 2], own.at[:, :, :, :, pl.ds(b * T, T)], out_sems.at[b]))
        outs[b].start()
    for copy in outs[-2:]:
        copy.wait()


def row_flag(ends, r):
    if r < WIDE:
        return ends[0]
    if r >= WIDE + ROWS:
        return ends[1]
    return None


def merge(fine):
    count = len(fine[0]) // 2
    sub = iota(fine[0][0].shape, 0)
    f0, f1, f2, f3 = fine[FIELDS : FIELDS + 4]
    inner = [f1[2 * p + 1] + f0[2 * p] for p in range(count)]
    coarse = []
    for f in range(FIELDS):
        both = [fine[f][2 * p] + fine[f][2 * p + 1] for p in range(count)]
        coarse.append([jnp.where(sub == f, both[p] - inner[p], both[p]) for p in range(count)])
    coarse.append([f0[2 * p + 1] for p in range(count)])
    coarse.append([f1[2 * p] for p in range(count)])
    coarse.append([f2[2 * p] + f2[2 * p + 1] for p in range(count)])
    coarse.append([f3[2 * p] + f3[2 * p + 1] for p in range(count)])
    return coarse


def build_levels(read, outs, sl, domain):
    fine = [[read(k, p) for p in range(PHASES)] for k in range(PLANES - 1)]
    for write in outs:
        fine = merge(fine)
        for p in range(len(fine[0])):
            weight = DAMP / diagonal([fine[f][p] for f in range(FIELDS)])
            if domain is not None:
                weight = jnp.where(domain > 0.0, weight, 0.0)
            if write is not None:
                for k, planes in enumerate(fine):
                    write(k, p, planes[p])
                write(SWEEP_W, p, weight)


def levels_kernel(ends, main, near, c1, c2):
    tiles = main.shape[-1] // T
    sides = side_domain(ends)

    def build(source, row, r, sl, domain):
        def put(out):
            def write(k, p, x):
                out[r, k, p, :, sl] = x

            return write

        build_levels(lambda k, p: source[row, k, p, :, sl], [put(c1), put(c2)], sl, domain)

    def body(r):
        each(tiles - 1, lambda j: build(main, r, r + WIDE, tile(j), None))

    each(ROWS, body)
    sl = slice((tiles - 1) * T, tiles * T)
    each(ROWS, lambda r: build(main, r, r + WIDE, sl, sides))
    for i, r in enumerate((1, EXT - 2)):
        each(tiles - 1, lambda j: build(near, i, r, tile(j), row_flag(ends, r)))
        build(near, i, r, sl, sides * row_flag(ends, r))


def far_planes(ends, rows, corners, wide, put):
    def fill(j):
        for i in range(2):
            cells = []
            for p in range(PHASES):
                planes = [rows[i, j, k * 8 : k * 8 + 8, p * T : p * T + T] for k in range(SENT - PLANES)]
                mask = planes[FIELDS][FIELDS:8] * ends[i]
                cells.append((planes[:FIELDS], planes[FIELDS:], planes, mask))
            put(i, cells, tile(j), ends[i])

    each(wide // T - 1, fill)
    for i in range(2):
        domain = side_domain(ends) * ends[i]
        planes, masks = corners[2 * i + 1]
        cells = []
        for p in range(PHASES):
            raw = [x[p] for x in planes]
            faces = raw[FIELDS : FIELDS + 4]
            mask = jnp.where(domain > 0.0, masks[p], 0.0)
            cells.append((with_face_sum(raw[:FIELDS], faces), [faces[0], faces[1], faces[2 + i]], raw[PLANES - 1], mask))
        put(i, cells, slice(wide - T, wide), domain)


def far_kernel(ends, rows_above, rows_below, corner_above, corner_below, order, order_side, far, order_out, rows):
    order_out[...] = natural_order()
    reorder_rows(rows_above, rows_below, slice(PLANES, SENT), order[...], rows)

    def put(i, cells, sl, domain):
        for p, (planes, faces, source, mask) in enumerate(cells):
            for k, x in enumerate(planes + faces[:2]):
                far[i, k, p, :, sl] = x
            far[i, FIELDS + 2 + i, p, :, sl] = faces[2]
            far[i, SWEEP_W, p, :, sl] = weight_of(planes, mask)
            far[i, SOURCE, p, :, sl] = last_sublanes(source) if isinstance(source, list) else source

    corners = corner_planes((corner_above, corner_below), order_side[...])
    far_planes(ends, rows, corners, far.shape[-1], put)


def far_coarse_kernel(ends, rows_above, rows_below, corner_above, corner_below, order, order_side, far, rows):
    reorder_rows(rows_above, rows_below, slice(PLANES, SENT), order[...], rows)

    def put(i, cells, sl, domain):
        def read(k, p):
            planes, faces, _, _ = cells[p]
            return planes[k] if k < FIELDS else faces[min(k - FIELDS, 2)]

        def write(k, p, x):
            if k in (FIELDS + 2, FIELDS + 3) and k != FIELDS + 2 + i:
                return
            far[i, k, p, :, sl] = x

        build_levels(read, [None, write], sl, domain)

    corners = corner_planes((corner_above, corner_below), order_side[...])
    far_planes(ends, rows, corners, far.shape[-1], put)


def apply_at(c, r, v, j, above=None, below=None):
    tiles = c.shape[-1] // T
    count = c.shape[2]
    sl = tile(j)
    before = tile(lax.rem(j + tiles - 1, tiles))
    after = tile(lax.rem(j + 1, tiles))
    lane = iota((8, T), 1)
    here = [v[r, p, :, sl] for p in range(count)]
    k = FIELDS
    east = [c[r, k, p, :, sl] * here[p] for p in range(count)]
    west = [c[r, k + 1, p, :, sl] * here[p] for p in range(count)]
    end = count - 1
    wrap = jnp.where(lane == T - 1, c[r, k, end, :, before] * v[r, end, :, before], east[end])
    from_left = [pltpu.roll(wrap, 1, 1)] + east[:end]
    wrap = jnp.where(lane == 0, c[r, k + 1, 0, :, after] * v[r, 0, :, after], west[0])
    from_right = west[1:] + [pltpu.roll(wrap, T - 1, 1)]
    outs = []
    for p in range(count):
        out = c[r, 0, p, :, sl] * v[r, p, 0:1, sl]
        for f in range(1, FIELDS):
            out = out + c[r, f, p, :, sl] * v[r, p, f : f + 1, sl]
        up = c[r - 1, k + 2, p, :, sl] * v[r - 1, p, :, sl] if above is None else above[p, :, sl]
        down = c[r + 1, k + 3, p, :, sl] * v[r + 1, p, :, sl] if below is None else below[p, :, sl]
        outs.append(out - (from_left[p] + from_right[p]) - (up + down))
    return outs


def smooth(c, t, old, new, first, last, above=None, below=None):
    def body(j):
        sl = tile(j)
        for r in range(first, last):
            up = above if r == first else None
            down = below if r == last - 1 else None
            for p, out in enumerate(apply_at(c, r, old, j, up, down)):
                diff = t[r, p, :, sl] - out
                new[r, p, :, sl] = old[r, p, :, sl] + diff * c[r, SWEEP_W, p, :, sl]

    each(c.shape[-1] // T, body)


def gather_rows(out, own, above, below, j, wide, weight=None):
    sl = tile(j)
    for r in range(WIDE - wide, WIDE + ROWS + wide):
        for p in range(out.shape[1]):
            if r < WIDE:
                val = above[WIDE - 1 - r, p, :, sl]
            elif r < WIDE + ROWS:
                val = own[r - WIDE, p, :, sl]
            else:
                val = below[r - WIDE - ROWS, p, :, sl]
            if weight is not None and not WIDE <= r < WIDE + ROWS:
                val = jnp.where(weight[r, SWEEP_W, p, :, sl] != 0.0, val, 0.0)
            out[r, p, :, sl] = val


def send_rows(top, bottom, row, p, sl, val, wide, product):
    if row < wide:
        top[row, p, :, sl] = val
    if row >= ROWS - wide:
        bottom[ROWS - 1 - row, p, :, sl] = val
    if row == wide:
        top[wide, p, :, sl] = product(FIELDS + 3)
    if row == ROWS - 1 - wide:
        bottom[wide, p, :, sl] = product(FIELDS + 2)


def reorder_rows(rows_above, rows_below, planes, order, out):
    blocks = rows_above.shape[-1] // BLOCK
    size = (planes.stop - planes.start) * 8
    parts = [rows[planes, :, b * BLOCK : b * BLOCK + BLOCK].reshape(size, BLOCK) for rows in (rows_above, rows_below) for b in range(blocks)]
    x = reorder(jnp.concatenate(parts, axis=0), order)
    for n in range(len(parts)):
        out[n // blocks, n % blocks] = x[n * size : n * size + size]


def first_kernel(ends, main, rows_above, rows_below, corner_above, corner_below, order, order_side, near, vb, t1, t1_top, t1_bottom, sums, va, prods, rows):
    tiles = main.shape[-1] // T
    c0 = FineRows(main, near)
    t0 = SourceOf(c0)
    last = slice((tiles - 1) * T, tiles * T)

    def put(i, p, planes, mask, sl):
        source = planes[PLANES - 1]
        weight = weight_of(planes[:FIELDS], mask)
        for k, x in enumerate(planes[: PLANES - 1] + [weight, source]):
            near[i, k, p, :, sl] = x
        va[1 if i == 0 else EXT - 2, p, :, sl] = weight * source

    def fill(j):
        sl = tile(j)
        for i in range(2):
            for p in range(PHASES):
                planes = [rows[i, j, k * 8 : k * 8 + 8, p * T : p * T + T] for k in range(PLANES)]
                put(i, p, planes, planes[PLANES - 1][FIELDS:8] * ends[i], sl)
                prods[i, p, :, sl] = last_sublanes(planes)

    reorder_rows(rows_above, rows_below, slice(0, PLANES), order[...], rows)
    each(tiles - 1, fill)
    sides = side_domain(ends)
    corners = corner_planes((corner_above, corner_below), order_side[...])
    for i in range(2):
        domain = sides * ends[i]
        planes, masks = corners[2 * i]
        far, far_masks = corners[2 * i + 1]
        for p in range(PHASES):
            raw = [x[p] for x in planes]
            raw[:FIELDS] = with_face_sum(raw[:FIELDS], raw[FIELDS : FIELDS + 4])
            put(i, p, raw, jnp.where(domain > 0.0, masks[p], 0.0), last)
            here = [x[p] for x in far]
            jac = with_face_sum(here[:FIELDS], here[FIELDS : FIELDS + 4])
            weight = weight_of(jac, jnp.where(domain > 0.0, far_masks[p], 0.0))
            prods[i, p, :, last] = here[FIELDS + 2 + i] * weight * here[PLANES - 1]

    def own(j):
        sl = tile(j)
        for r in range(WIDE, WIDE + ROWS):
            for p in range(PHASES):
                va[r, p, :, sl] = c0[r, SWEEP_W, p, :, sl] * t0[r, p, :, sl]

    each(tiles, own)

    smooth(c0, t0, va, vb, 1, EXT - 1, prods.at[0], prods.at[1])
    sums[...] = jnp.zeros_like(sums)

    def rest(j):
        sl = tile(j)
        total = jnp.zeros((8, T), F32)
        for r in range(WIDE, WIDE + ROWS):
            res = []
            for p, out in enumerate(apply_at(c0, r, vb, j)):
                diff = t0[r, p, :, sl] - out
                res.append(jnp.where(c0[r, SWEEP_W, p, :, sl] != 0.0, diff, 0.0))
                total = total + res[p] * res[p]
            row = r - WIDE
            if row in (1, ROWS - 2):
                coarse = merge([[c0[r, k, p, :, sl] for p in range(PHASES)] for k in range(PLANES - 1)])
            for p in range(PHASES // 2):
                val = res[2 * p] + res[2 * p + 1]
                t1[row, p, :, sl] = val

                def product(k):
                    diag = diagonal([coarse[f][p] for f in range(FIELDS)])
                    return coarse[k][p] * jnp.where(diag > 0.0, DAMP / diag, 0.0) * val

                send_rows(t1_top, t1_bottom, row, p, sl, val, 1, product)
        sums[...] += jnp.where(j < tiles - 1, total, 0.0)

    each(tiles, rest)


def second_kernel(c1, c2, t1_own, above, below, t1, vb, t2, top, bottom, sums, va):
    tiles = c1.shape[-1] // T

    def fill(j):
        sl = tile(j)
        gather_rows(t1, t1_own, above, below, j, 1)
        for r in range(1, EXT - 1):
            for p in range(2):
                va[r, p, :, sl] = c1[r, SWEEP_W, p, :, sl] * t1[r, p, :, sl]

    each(tiles, fill)
    smooth(c1, t1, va, vb, 1, EXT - 1, above.at[1], below.at[1])
    sums[...] = jnp.zeros_like(sums)

    def rest(j):
        sl = tile(j)
        total = jnp.zeros((8, T), F32)
        for r in range(WIDE, WIDE + ROWS):
            res = [t1[r, p, :, sl] - out for p, out in enumerate(apply_at(c1, r, vb, j))]
            total = total + res[0] * res[0] + res[1] * res[1]
            val = res[0] + res[1]
            t2[r - WIDE, 0, :, sl] = val

            def product(k):
                return c2[r, k, 0, :, sl] * c2[r, SWEEP_W, 0, :, sl] * val

            send_rows(top, bottom, r - WIDE, 0, sl, val, WIDE, product)
        sums[...] += jnp.where(j < tiles - 1, total, 0.0)

    each(tiles, rest)


def third_kernel(main, c1, far, t2_own, above, below, e1_in, e1, top, bottom, t2, va, vb):
    tiles = main.shape[-1] // T
    c2 = WithFar(main, far)

    def fill(j):
        sl = tile(j)
        gather_rows(t2, t2_own, above, below, j, WIDE)
        for r in range(EXT):
            va[r, 0, :, sl] = c2[r, SWEEP_W, 0, :, sl] * t2[r, 0, :, sl]

    each(tiles, fill)
    smooth(c2, t2, va, vb, 0, EXT, above.at[WIDE], below.at[WIDE])
    smooth(c2, t2, vb, va, 1, EXT - 1)
    smooth(c2, t2, va, vb, WIDE, WIDE + ROWS)

    def last(j):
        sl = tile(j)
        for r in range(WIDE, WIDE + ROWS):
            for p in range(2):
                val = e1_in[r, p, :, sl] + vb[r, 0, :, sl]
                e1[r - WIDE, p, :, sl] = val
                send_rows(top, bottom, r - WIDE, p, sl, val, 1, lambda k: c1[r, k, p, :, sl] * val)

    each(tiles, last)


def fourth_kernel(c1, main, t1, e1, above, below, v2, v, top, bottom, va, vb):
    tiles = c1.shape[-1] // T
    each(tiles, lambda j: gather_rows(va, e1, above, below, j, 1, c1))
    smooth(c1, t1, va, vb, 1, EXT - 1, above.at[1], below.at[1])
    smooth(c1, t1, vb, va, WIDE, WIDE + ROWS)

    def last(j):
        sl = tile(j)
        for r in range(ROWS):
            for p in range(PHASES):
                add = jnp.where(main[r, SWEEP_W, p, :, sl] != 0.0, va[r + WIDE, p // 2, :, sl], 0.0)
                val = v2[r + WIDE, p, :, sl] + add
                v[r, p, :, sl] = val
                send_rows(top, bottom, r, p, sl, val, WIDE, lambda k: main[r, k, p, :, sl] * val)

    each(tiles, last)


def fifth_kernel(main, near, far, v, above, below, order, adjoint, residual, sums, va, vb, buf):
    tiles = main.shape[-1] // T
    c0 = FineRows(main, near, far)
    t0 = SourceOf(c0)
    each(tiles, lambda j: gather_rows(va, v, above, below, j, WIDE, c0))
    smooth(c0, t0, va, vb, 0, EXT, above.at[WIDE], below.at[WIDE])
    smooth(c0, t0, vb, va, 1, EXT - 1)
    sums[...] = jnp.zeros_like(sums)

    def rest(j):
        sl = tile(j)
        total = jnp.zeros((8, T), F32)
        for r in range(WIDE, WIDE + ROWS):
            for p, out in enumerate(apply_at(c0, r, va, j)):
                diff = t0[r, p, :, sl] - out
                res = jnp.where(c0[r, SWEEP_W, p, :, sl] != 0.0, diff, 0.0)
                total = total + res * res
                buf[j, p, pl.ds(r - WIDE, FIELDS, stride=ROWS), :] = va[r, p, 0:FIELDS, sl]
                buf[j, p, pl.ds(GRID + r - WIDE, FIELDS, stride=ROWS), :] = res[0:FIELDS]
        sums[...] += total

    each(tiles - 1, rest)
    x = jnp.concatenate([jnp.concatenate([buf[j, p] for p in range(PHASES)], axis=1) for j in range(tiles - 1)], axis=0)
    y = reorder(x, order[...])
    for j in range(tiles - 1):
        cols = slice(j * BLOCK, j * BLOCK + BLOCK)
        adjoint[:, cols] = y[2 * j * GRID : (2 * j + 1) * GRID]
        residual[:, cols] = y[(2 * j + 1) * GRID : (2 * j + 2) * GRID]


def call(kernel, outs, args, scratch=(), spaces=None, size=0, limit=LIMIT, out_spaces=None):
    spaces = spaces or {}
    return pl.pallas_call(
        kernel,
        out_shape=[jax.ShapeDtypeStruct(s, F32) if isinstance(s, tuple) else s for s in outs],
        in_specs=[pl.BlockSpec(memory_space=spaces.get(i, pltpu.VMEM)) for i in range(len(args))],
        out_specs=[pl.BlockSpec(memory_space=(out_spaces or {}).get(i, pltpu.VMEM)) for i in range(len(outs))],
        scratch_shapes=[pltpu.VMEM(s, F32) if isinstance(s, tuple) else s for s in scratch],
        compiler_params=pltpu.CompilerParams(vmem_limit_bytes=limit),
        cost_estimate=pl.CostEstimate(flops=0, bytes_accessed=size, transcendentals=0),
        name=kernel.__name__,
    )(*args)


def ring(x, axis, step):
    count = lax.axis_size(axis)
    return lax.ppermute(x, axis, [(i, (i + step) % count) for i in range(count)])


def total_over_devices(x):
    axes = ("hull", "blk")
    count = lax.axis_size(axes)
    sent = jnp.broadcast_to(jnp.pad(x, (0, T - x.size))[None], (count, T))
    return jnp.sum(lax.all_to_all(sent, axes, 0, 0, tiled=True), axis=0)[: x.size]


def on_device(source, jacobian, face_coef, active):
    columns = source.shape[2]
    quads = columns // PHASES
    wide = quads + T
    blocks = columns // BLOCK
    hull, blk = lax.axis_index("hull"), lax.axis_index("blk")
    ends = jnp.stack([hull > 0, hull < lax.axis_size("hull") - 1, blk > 0, blk < lax.axis_size("blk") - 1]).astype(F32)

    def cells(rows, phases):
        return (rows, phases, 8, wide)

    def coefs(rows, planes, phases):
        return (rows, planes, phases, 8, wide)

    flag = {0: pltpu.SMEM}
    inputs = [
        jacobian.reshape(FIELDS, GRID, columns),
        face_coef.reshape(4, GRID, columns),
        source.reshape(GRID, columns),
        active,
    ]
    in_hbm = {i: pltpu.HBM for i in range(len(inputs))}
    tiles = columns // T
    staged = [(tiles, FIELDS, GRID, T), (tiles, 4, GRID, T), (tiles, GRID, T), pltpu.VMEM((ROWS, columns), jnp.int32)]
    order = jax.ShapeDtypeStruct((BLOCK, BLOCK), BF16)
    order_side = jax.ShapeDtypeStruct((2 * T, BLOCK), BF16)
    sum_tile = (8, T)

    rows = pltpu.HBM((SENT, 8, columns), F32)
    top, bottom, left, right = call(
        send_kernel,
        [rows, rows] + [(PACK + ROWS, T)] * 2,
        [pltpu.with_memory_space_constraint(x, pltpu.HBM) for x in inputs],
        [*staged, (2, SENT, 8, columns), pltpu.SemaphoreType.DMA((tiles, 4)), pltpu.SemaphoreType.DMA((blocks, 2))],
        in_hbm,
        limit=12 * 2**20,
        out_spaces={0: pltpu.HBM, 1: pltpu.HBM},
    )
    from_right = ring(left, "blk", -1)
    from_left = ring(right, "blk", 1)
    rows_below = ring(top, "hull", -1)
    rows_above = ring(bottom, "hull", 1)
    inner, token = call(
        own_kernel,
        [pltpu.HBM((ROWS, FINE, PHASES, 8, quads), F32), sum_tile],
        inputs,
        [
            pltpu.VMEM((BLOCK, BLOCK), BF16),
            (2, PHASES, RAW, T),
            (2, PHASES, ROWS, T),
            (2, ROWS, FINE, PHASES, 8, T),
            pltpu.SemaphoreType.DMA((blocks,)),
        ],
        size=25 * 10**6,
        limit=16 * 2**20,
        out_spaces={0: pltpu.HBM},
    )
    inner = pltpu.with_memory_space_constraint(inner, pltpu.HBM)
    corner = (2, 2, PER_GROUP * 8, T)
    top, bottom = call(corner_kernel, [corner, corner], [from_right, from_left, token], spaces={2: pl.ANY})
    corner_below = ring(top, "hull", -1)
    corner_above = ring(bottom, "hull", 1)
    main, own, side = call(
        side_kernel,
        [coefs(ROWS, FINE, 4), order, order_side],
        [ends, from_right, from_left, inner],
        [(PHASES, RAW, T), (PHASES, ROWS, T), pltpu.SemaphoreType.DMA((ROWS,))],
        {0: pltpu.SMEM, 3: pltpu.HBM},
        size=9 * 10**6,
    )
    near, v2, t1, top, bottom, sum0 = call(
        first_kernel,
        [coefs(2, FINE, 4), cells(EXT, 4), cells(ROWS, 2), cells(2, 2), cells(2, 2), sum_tile],
        [ends, main, rows_above, rows_below, corner_above, corner_below, own, side],
        [cells(EXT, 4), cells(2, 4), (2, blocks, PLANES * 8, BLOCK)],
        flag,
    )
    below = ring(top, "hull", -1)
    above = ring(bottom, "hull", 1)
    (far2,) = call(
        far_coarse_kernel,
        [coefs(2, PLANES, 1)],
        [ends, rows_above, rows_below, corner_above, corner_below, own, side],
        [(2, blocks, (SENT - PLANES) * 8, BLOCK)],
        flag,
        size=7 * 10**6,
    )
    far, natural = call(
        far_kernel,
        [coefs(2, FINE, 4), order],
        [ends, rows_above, rows_below, corner_above, corner_below, own, side],
        [(2, blocks, (SENT - PLANES) * 8, BLOCK)],
        flag,
        size=8 * 10**6,
    )
    c1, c2 = call(levels_kernel, [coefs(EXT, PLANES, 2), coefs(EXT, PLANES, 1)], [ends, main, near], (), flag, size=10**7)
    t1, e1, t2, top, bottom, sum1 = call(
        second_kernel,
        [cells(EXT, 2), cells(EXT, 2), cells(ROWS, 1), cells(3, 1), cells(3, 1), sum_tile],
        [c1, c2, t1, above, below],
        [cells(EXT, 2)],
    )
    below = ring(top, "hull", -1)
    above = ring(bottom, "hull", 1)
    e1, top, bottom = call(
        third_kernel,
        [cells(ROWS, 2), cells(2, 2), cells(2, 2)],
        [c2, c1, far2, t2, above, below, e1],
        [cells(EXT, 1)] * 3,
    )
    below = ring(top, "hull", -1)
    above = ring(bottom, "hull", 1)
    v, top, bottom = call(
        fourth_kernel, [cells(ROWS, 4), cells(3, 4), cells(3, 4)], [c1, main, t1, e1, above, below, v2], [cells(EXT, 2)] * 2
    )
    below = ring(top, "hull", -1)
    above = ring(bottom, "hull", 1)
    adjoint, residual, sum2 = call(
        fifth_kernel,
        [(GRID, columns), (GRID, columns), sum_tile],
        [main, near, far, v, above, below, natural],
        [cells(EXT, 4)] * 2 + [(blocks, PHASES, 2 * GRID, T)],
    )
    squares = jnp.stack([sum0, 2.0 * sum1, sum2])
    squares = total_over_devices(jnp.sum(squares[:, :FIELDS], axis=(1, 2)))
    count = source.size * lax.axis_size("hull") * lax.axis_size("blk")
    level_rms = jnp.sqrt(squares / float(count))
    return adjoint.reshape(source.shape), residual.reshape(source.shape), level_rms


def solution(mesh):
    return jax.shard_map(
        on_device,
        mesh=mesh,
        in_specs=(
            P(None, "hull", "blk"),
            P(None, None, "hull", "blk"),
            P(None, None, "hull", "blk"),
            P("hull", "blk"),
        ),
        out_specs=(P(None, "hull", "blk"), P(None, "hull", "blk"), P()),
        check_vma=False,
    )
```
